256 devices in a mesh: basin: 128 (over x, y, z), rep: 2 (over core).
Axes of the slice: x: 4, y: 4, z: 8, core: 2. Of those that a mesh axis runs over, the one named last changes fastest.
Arguments:
- forcing: bfloat16 [16, 32, 65536], P(None, None, ('basin', 'rep')), may hold values from -6 to 6
- w_in: bfloat16 [1024, 32], replicated, may hold values from -1 to 1
- w_rec: bfloat16 [1024, 256], replicated, may hold values from -0.375 to 0.375
- bias: float32 [1024], replicated, may hold values from -3 to 3
- w_out: float32 [256], replicated, may hold values from -0.375 to 0.375
- uh_shape: float32 [65536], P(('basin', 'rep')), may hold values from 1.5 to 4
- uh_scale: float32 [65536], P(('basin', 'rep')), may hold values from 0.5 to 4
- reach_tier: int32 [65536], P(('basin', 'rep')), may hold values from 0 to 3, as said below
- reach_dest: int32 [65536], P(('basin', 'rep')), may hold values from -1 to 65535, as said below
- out_cot: float32 [16, 65536], P(None, ('basin', 'rep')), may hold values from -0.0625 to 0.0625
Outputs:
- outflow: float32 [16, 65536], P(None, ('basin', 'rep'))
- grad_w_in: float32 [1024, 32], replicated
- grad_w_rec: float32 [1024, 256], replicated
- grad_bias: float32 [1024], replicated
- grad_w_out: float32 [256], replicated
The draws below stay inside these ranges and needn't reach their ends.
Inputs may be any that keep to these rules, and one draw needn't show every extreme that they name: `reach_tier`: every device holds reaches of every tier. `reach_dest`: -1 for a reach that leaves the network (all reaches of tier 4 - 1 among them); else the global index of a reach of the next tier on a device with the same rep index and a basin index from the own to the own + 2; of one device's reaches of one tier, at most 8 drain into reaches of one device, and on every device 8 reaches of tier 0 drain into its own reaches.
All inputs are finite; a program needn't handle non-finite values.
Results may differ from the reference program's by a relative error of at most 0.0034.
Values sent between devices are 32-bit elements; how exact they have to be, the bound alone decides.
A program may use at most 128 MiB of HBM per device.

```python
import math
import jax
import jax.numpy as jnp
from jax import lax

HID = 256
FEAT = 32
REACH_DEV = 256
DAYS = 16
UHLEN = 8
LEVELS = 4
CAP = 8
SPREAD = 3
REACHES = 65536
N_BASIN = 128
N_REP = 2


def river_links(key):
    devices = N_BASIN * N_REP
    key_tier, key_offset, key_pick = jax.random.split(key, 3)
    local = jnp.arange(REACH_DEV, dtype=jnp.int32)[None, :]
    tiers = jax.random.randint(key_tier, (devices, REACH_DEV), 0, LEVELS).astype(jnp.int32)
    forced = (local >= LEVELS) & (local < LEVELS + CAP)
    tiers = jnp.where(local < LEVELS, local, jnp.where(forced, 0, tiers))
    offsets = jax.random.randint(key_offset, (devices, REACH_DEV), 0, SPREAD).astype(jnp.int32)
    offsets = jnp.where(forced, 0, jnp.where(local < LEVELS, 1, offsets))
    device = jnp.arange(devices, dtype=jnp.int32)[:, None]
    basin_index = device // N_REP
    rep_index = device % N_REP
    target_basin = jnp.minimum(basin_index + offsets, N_BASIN - 1)
    placed = target_basin - basin_index
    key_ids = tiers * SPREAD + placed
    onehot = (key_ids[:, :, None] == jnp.arange(LEVELS * SPREAD, dtype=jnp.int32)[None, None, :]).astype(jnp.int32)
    slot_rank = jnp.sum((jnp.cumsum(onehot, axis=1) - onehot) * onehot, axis=2)
    keep = (slot_rank < CAP) & (tiers < LEVELS - 1)
    target_device = target_basin * N_REP + rep_index
    candidate_tiers = tiers[target_device]
    scores = jax.random.randint(key_pick, (devices, REACH_DEV, REACH_DEV), 0, 65536).astype(jnp.int32) * REACH_DEV + local[None]
    scores = jnp.where(candidate_tiers == tiers[:, :, None] + 1, scores, -1)
    picked = jnp.argmax(scores, axis=2).astype(jnp.int32)
    dest = jnp.where(keep, target_device * REACH_DEV + picked, -1)
    return (tiers.reshape(-1).astype(jnp.int32), dest.reshape(-1).astype(jnp.int32))


def draw_reach_tier(key, part):
    return river_links(key)[0]


def draw_reach_dest(key, part):
    return river_links(key)[1]


def levels(stream_key, extent, pieces, smallest, top_value):
    factor_of, own = 1.0, jax.random.fold_in(stream_key, 6)
    for dim, parts in pieces:
        heights = jnp.exp(jax.random.uniform(jax.random.fold_in(own, dim), (parts,), jnp.float32, smallest / len(pieces), top_value / len(pieces)))
        factor_of = factor_of * jnp.repeat(heights, extent[dim] // parts).reshape([-1 if axis == dim else 1 for axis in range(len(extent))])
    return factor_of


def gaussian(own_key, dims, spread, limit, cuts=(), kind=jnp.bfloat16):
    entries = jax.random.normal(own_key, dims, jnp.float32) * spread
    if len(cuts) > 0:
        entries = levels(own_key, dims, cuts, -0.22, 0.18) * entries
    return jnp.clip(entries, min=-limit, max=limit).astype(kind)


def setup_inputs(seed: int = 0) -> dict:
    streams_of = jax.random.split(jax.random.key(seed), 11)
    return {
        "forcing": gaussian(streams_of[0], (DAYS, FEAT, REACHES), 1.0, 6.0, ((2, 256),)),
        "w_in": gaussian(streams_of[1], (4 * HID, FEAT), FEAT ** -0.5, 1.0),
        "w_rec": gaussian(streams_of[2], (4 * HID, HID), HID ** -0.5, 0.375),
        "bias": gaussian(streams_of[3], (4 * HID,), 0.5, 3.0, (), jnp.float32),
        "w_out": gaussian(streams_of[4], (HID,), HID ** -0.5, 0.375, (), jnp.float32),
        "uh_shape": jnp.clip(jnp.exp(math.log(4.0) - 0.98082925 * jax.random.uniform(streams_of[5], (REACHES,), jnp.float32) ** levels(streams_of[5], (REACHES,), ((0, 256),), -0.2, 0.2)), 1.5, 4.0),
        "uh_scale": jnp.clip(jnp.exp(math.log(4.0) - 2.0794415 * jax.random.uniform(streams_of[6], (REACHES,), jnp.float32) ** levels(streams_of[6], (REACHES,), ((0, 256),), -0.2, 0.2)), 0.5, 4.0),
        "reach_tier": draw_reach_tier(jax.random.fold_in(streams_of[10], 71), 0),
        "reach_dest": draw_reach_dest(jax.random.fold_in(streams_of[10], 71), 0),
        "out_cot": gaussian(streams_of[9], (DAYS, REACHES), (4.0 / (REACHES * DAYS) ** 0.5), 0.0625, ((1, 256),), jnp.float32),
    }


def hydro_kernel(uh_shape, uh_scale, length):
    lag_days = (jnp.arange(length, dtype=jnp.float32) + 1.0)[:, None]
    weights = jnp.exp((uh_shape[None, :] - 1.0) * jnp.log(lag_days) - lag_days / uh_scale[None, :])
    return weights / jnp.sum(weights, axis=0, keepdims=True)


def convolve(kernel, series):
    length = kernel.shape[0]
    day_count = series.shape[0]
    padded = jnp.concatenate([jnp.zeros((length - 1, series.shape[1]), jnp.float32), series], 0)
    summed = jnp.zeros_like(series)
    for lag_index in range(length):
        start = length - 1 - lag_index
        summed = summed + kernel[lag_index][None, :] * padded[start:start + day_count]
    return summed


def correlate(kernel, series):
    length = kernel.shape[0]
    day_count = series.shape[0]
    padded = jnp.concatenate([series, jnp.zeros((length - 1, series.shape[1]), jnp.float32)], 0)
    summed = jnp.zeros_like(series)
    for lag_index in range(length):
        summed = summed + kernel[lag_index][None, :] * padded[lag_index:lag_index + day_count]
    return summed


def lstm_forward(forcing, w_in, w_rec, bias, w_out):
    width = w_rec.shape[1]
    reaches = forcing.shape[2]

    def step(state_pair, forcing_now):
        state_h, state_c = state_pair
        h_low = state_h.astype(jnp.bfloat16)
        preact = jnp.dot(w_in, forcing_now, preferred_element_type=jnp.float32)
        preact = preact + jnp.dot(w_rec, h_low, preferred_element_type=jnp.float32) + bias[:, None]
        gate_i = jax.nn.sigmoid(preact[:width])
        gate_f = jax.nn.sigmoid(preact[width:2 * width])
        gate_g = jnp.tanh(preact[2 * width:3 * width])
        gate_o = jax.nn.sigmoid(preact[3 * width:])
        cell_now = gate_f * state_c + gate_i * gate_g
        hidden = gate_o * jnp.tanh(cell_now)
        readout = jnp.dot(w_out, hidden, precision=lax.Precision.HIGHEST)
        return (hidden, cell_now), (jax.nn.softplus(readout), h_low, state_c, cell_now, gate_i, gate_f, gate_g, gate_o, readout)

    zeros = jnp.zeros((width, reaches), jnp.float32)
    _, saved = lax.scan(step, (zeros, zeros), forcing)
    return saved


def lstm_backward(forcing, w_rec, w_out, saved, grad_runoff):
    width = w_rec.shape[1]
    reaches = forcing.shape[2]
    _, h_low, cell_prev, cell_all, gate_i, gate_f, gate_g, gate_o, readout = saved

    def step(state_pair, inputs_now):
        grad_h_next, grad_c_next, acc_in, acc_rec, acc_bias, acc_out = state_pair
        forcing_now, hl_now, cp_now, ce_now, gi_now, gf_now, gg_now, go_now, read_now, gq_now = inputs_now
        grad_read = jax.nn.sigmoid(read_now) * gq_now
        tanh_c = jnp.tanh(ce_now)
        hidden = go_now * tanh_c
        acc_out = acc_out + jnp.dot(hidden, grad_read, precision=lax.Precision.HIGHEST)
        grad_h = w_out[:, None] * grad_read[None, :] + grad_h_next
        grad_c = grad_h * go_now * (1.0 - tanh_c * tanh_c) + grad_c_next
        grad_z = jnp.concatenate([grad_c * gg_now * gi_now * (1.0 - gi_now),
                                  grad_c * cp_now * gf_now * (1.0 - gf_now),
                                  grad_c * gi_now * (1.0 - gg_now * gg_now),
                                  grad_h * tanh_c * go_now * (1.0 - go_now)], 0)
        grad_z_low = grad_z.astype(jnp.bfloat16)
        acc_in = acc_in + jnp.dot(grad_z_low, forcing_now.T, preferred_element_type=jnp.float32)
        acc_rec = acc_rec + jnp.dot(grad_z_low, hl_now.T, preferred_element_type=jnp.float32)
        acc_bias = acc_bias + jnp.sum(grad_z, axis=1)
        grad_h_prev = jnp.dot(w_rec.T, grad_z_low, preferred_element_type=jnp.float32)
        return (grad_h_prev, grad_c * gf_now, acc_in, acc_rec, acc_bias, acc_out), None

    zeros = jnp.zeros((width, reaches), jnp.float32)
    start_state = (zeros, zeros,
                   jnp.zeros((4 * width, forcing.shape[1]), jnp.float32),
                   jnp.zeros((4 * width, width), jnp.float32),
                   jnp.zeros((4 * width,), jnp.float32),
                   jnp.zeros((width,), jnp.float32))
    inputs_all = (forcing, h_low, cell_prev, cell_all, gate_i, gate_f, gate_g, gate_o, readout, grad_runoff)
    final_state, _ = lax.scan(step, start_state, inputs_all, reverse=True)
    return final_state[2], final_state[3], final_state[4], final_state[5]


def reference(forcing, w_in, w_rec, bias, w_out, uh_shape, uh_scale, reach_tier, reach_dest, out_cot):
    block_size = REACH_DEV * min(16, N_BASIN * N_REP)
    block_count = (REACH_DEV * N_BASIN * N_REP) // block_size
    blocks = jnp.moveaxis(forcing.reshape(DAYS, FEAT, block_count, block_size), 2, 0)

    def block_runoff(block_forcing):
        return lstm_forward(block_forcing, w_in, w_rec, bias, w_out)[0]

    runoff_blocks = lax.map(block_runoff, blocks)
    runoff = jnp.moveaxis(runoff_blocks, 0, 1).reshape(DAYS, block_count * block_size)
    kernel = hydro_kernel(uh_shape, uh_scale, UHLEN)
    linked = reach_dest >= 0
    target = jnp.where(linked, reach_dest, 0).astype(jnp.int32)
    inflow = jnp.zeros_like(runoff)
    for tier_now in range(LEVELS - 1):
        flow_now = convolve(kernel, runoff + inflow)
        outgoing = jnp.where((linked & (reach_tier == tier_now))[None, :], flow_now, jnp.float32(0.0))
        inflow = inflow.at[:, target].add(outgoing)
    outflow = convolve(kernel, runoff + inflow)
    grad_out = out_cot
    for tier_now in range(LEVELS - 2, -1, -1):
        grad_in = correlate(kernel, grad_out)
        returning = jnp.where((linked & (reach_tier == tier_now))[None, :], grad_in[:, target], jnp.float32(0.0))
        grad_out = grad_out + returning
    grad_runoff = correlate(kernel, grad_out)
    grad_blocks = jnp.moveaxis(grad_runoff.reshape(DAYS, block_count, block_size), 1, 0)

    def accumulate(totals, inputs_now):
        block_forcing, block_grad = inputs_now
        saved = lstm_forward(block_forcing, w_in, w_rec, bias, w_out)
        terms = lstm_backward(block_forcing, w_rec, w_out, saved, block_grad)
        return tuple(first + second for first, second in zip(totals, terms)), None

    start_totals = (jnp.zeros((4 * HID, FEAT), jnp.float32), jnp.zeros((4 * HID, HID), jnp.float32),
                    jnp.zeros((4 * HID,), jnp.float32), jnp.zeros((HID,), jnp.float32))
    totals, _ = lax.scan(accumulate, start_totals, (blocks, grad_blocks))
    return (outflow, totals[0], totals[1], totals[2], totals[3])
```

```python
import jax
import jax.numpy as jnp
from jax import lax
from jax.experimental import pallas as pl
from jax.experimental.pallas import tpu as pltpu
from jax.sharding import PartitionSpec as P

MESH = pl.DeviceIdType.MESH
VMEM = pltpu.VMEM
f32 = jnp.float32
bf16 = jnp.bfloat16
DAYS = 16
HID = 256
FEAT = 32
REACH = 256
UHLEN = 8
XROWS = 304
GROWS = 1040
CHUNK = 32
SEMS = 200
NT = (((1,), (1,)), ((), ()))


class Place:
    def __init__(self):
        self.b = lax.axis_index("basin")
        self.r = lax.axis_index("rep")
        self.x = self.b // 32
        self.y = (self.b // 8) % 4
        self.z = self.b % 8
        self.q = self.x * 4 + self.y

    def core(self):
        return (self.b, 1 - self.r)

    def plane(self, d):
        px = lax.rem(self.x + d // 4, 4)
        py = lax.rem(self.y + d % 4, 4)
        return (px * 32 + py * 8 + self.z, self.r), px * 4 + py

    def plane_from(self, d):
        return lax.rem(self.x + 4 - d // 4, 4) * 4 + lax.rem(self.y + 4 - d % 4, 4)

    def line(self, d):
        pz = lax.rem(self.z + d, 8)
        return (self.x * 32 + self.y * 8 + pz, self.r), pz

    def line_from(self, d):
        return lax.rem(self.z + 8 - d, 8)

    def along(self, d):
        return (lax.rem(self.b + 128 + d, 128), self.r)


class Copies:
    def __init__(self, send, recv):
        self.send = send
        self.recv = recv
        self.all = []

    def __call__(self, src, dst, device):
        i = len(self.all)
        copy = pltpu.make_async_remote_copy(
            src_ref=src,
            dst_ref=dst,
            send_sem=self.send.at[i],
            recv_sem=self.recv.at[i],
            device_id=device,
            device_id_type=MESH,
        )
        copy.start()
        self.all.append(copy)
        return copy

    def drain(self):
        for copy in self.all:
            copy.wait_send()


def rows(start, size):
    return pl.ds(pl.multiple_of(start, 8), size)


def split3(v):
    hi = v.astype(bf16).astype(f32)
    mid = (v - hi).astype(bf16).astype(f32)
    return hi, mid, v - hi - mid


def hydro(shape_row, scale_row):
    lag = lax.broadcasted_iota(jnp.int32, (UHLEN, REACH), 0).astype(f32) + 1.0
    u = jnp.exp((shape_row - 1.0) * jnp.log(lag) - lag / scale_row)
    return u / jnp.sum(u, axis=0, keepdims=True)


def convolve(uh, series, pad):
    pad[8:24] = series
    total = uh[0:1] * series
    for m in range(1, UHLEN):
        total = total + uh[m : m + 1] * pad[8 - m : 24 - m]
    return total


def correlate(uh, series, pad):
    pad[8:24] = series
    total = uh[0:1] * series
    for m in range(1, UHLEN):
        total = total + uh[m : m + 1] * pad[8 + m : 24 + m]
    return total


def gather(blocks, index):
    halves = []
    for h in range(2):
        idx = jnp.broadcast_to(index[:, h * 128 : (h + 1) * 128], (DAYS, 128))
        lane = jnp.bitwise_and(idx, 127)
        block = jnp.right_shift(idx, 7)
        total = jnp.zeros((DAYS, 128), f32)
        for i in range(6):
            source = blocks[i // 2][:, (i % 2) * 128 : (i % 2 + 1) * 128]
            picked = jnp.take_along_axis(source, lane, axis=1)
            total = jnp.where(block == i, picked, total)
        halves.append(total)
    return jnp.concatenate(halves, 1)


def kernel(
    forcing, w_in_t, w_rec, bias, w_out, uh_shape, uh_scale, dest, cot,
    o_flow, o_in, o_rec, o_bias, o_out,
    W, WT, wcol, x, gates, cells, gz, gh, gcn, rd, grd,
    accA, accB, pad, adj, par, parb, route, fS, fR,
    bufA, rsA, zA, bufB, zB, xyB, outB, send, recv,
):
    p = Place()
    cp = Copies(send, recv)

    barrier = pltpu.get_barrier_semaphore()
    partners = [p.core()]
    partners += [p.plane(d)[0] for d in range(1, 16)]
    partners += [p.line(d)[0] for d in range(1, 8)]
    partners += [p.along(d) for d in (1, 2, 3, 4, 5, 6, -1, -2, -3, -4, -5, -6)]
    for device in partners:
        pl.semaphore_signal(barrier, inc=1, device_id=device, device_id_type=MESH)

    pad[...] = jnp.zeros_like(pad)
    uh = hydro(uh_shape[...], uh_scale[...])
    dest_row = dest[...]
    linked = dest_row >= 0
    ahead = jnp.right_shift(dest_row, 9) - p.b
    index = jnp.where(linked, ahead * REACH + jnp.bitwise_and(dest_row, REACH - 1), -1)
    row8 = lax.broadcasted_iota(jnp.int32, (8, REACH), 0)
    par[0] = jnp.where(
        row8 == 0, uh_shape[...], jnp.where(row8 == 1, uh_scale[...], index.astype(f32))
    )
    adj[0] = correlate(uh, cot[...], pad)

    for k in range(0, 1024, 128):
        half = 0.5 if k // 256 == 2 else 0.25
        back = 0.25 if k // 256 >= 2 else 0.125
        block = w_rec[k : k + 128].astype(f32)
        W[k : k + 128, 0:256] = (block * half).astype(bf16)
        WT[:, k : k + 128] = (block.T * back).astype(bf16)
        part = w_in_t[:, k : k + 128].astype(f32) * (2.0 * half)
        hi, mid, lo = split3(bias[:, k : k + 128] * (2.0 * half))
        row = lax.broadcasted_iota(jnp.int32, (96, 128), 0)
        rest = jnp.where(row == 0, hi, jnp.where(row == 1, mid, jnp.where(row == 2, lo, 0.0)))
        W[k : k + 128, 256:304] = jnp.concatenate([part, rest], 0).T[:, 0:48].astype(bf16)
    row16 = lax.broadcasted_iota(jnp.int32, (16, REACH), 0)
    hi, mid, lo = split3(w_out[...] * 0.5)
    W[1024:1040, 0:256] = jnp.where(
        row16 == 0, hi, jnp.where(row16 == 1, mid, jnp.where(row16 == 2, lo, 0.0))
    ).astype(bf16)
    W[1024:1040, 256:304] = jnp.zeros((16, 48), bf16)
    wcol[...] = jnp.broadcast_to(w_out[...], (128, HID)).T

    x[0, 0:256] = jnp.zeros((HID, REACH), bf16)
    ones = jnp.where(row16 < 3, 1.0, 0.0).astype(bf16)
    for t in range(DAYS):
        x[t, 256:288] = forcing[t]
        x[t, 288:304] = ones
    x[DAYS, 256:304] = jnp.zeros((48, REACH), bf16)
    cells[0] = jnp.zeros((HID, REACH), f32)

    def forward(t, _):
        pre = jnp.dot(W[...], x[t], preferred_element_type=f32)
        rd[pl.ds(t, 1)] = jnp.sum(pre[1024:1032], axis=0, keepdims=True)
        for c in range(0, HID, CHUNK):
            s = pl.ds(c, CHUNK)
            ti = jnp.tanh(pre[c : c + CHUNK])
            tf = jnp.tanh(pre[HID + c : HID + c + CHUNK])
            tg = jnp.tanh(pre[2 * HID + c : 2 * HID + c + CHUNK])
            to = jnp.tanh(pre[3 * HID + c : 3 * HID + c + CHUNK])
            cell = 0.5 * ((tf + 1.0) * cells[t, s] + (ti + 1.0) * tg)
            gates[0, t, s] = ti
            gates[1, t, s] = tf
            gates[2, t, s] = tg
            gates[3, t, s] = to
            cells[t + 1, s] = cell
            x[t + 1, s] = ((to + 1.0) * jnp.tanh(cell)).astype(bf16)
        return 0

    lax.fori_loop(0, 6, forward, 0)

    pl.semaphore_wait(barrier, len(partners))
    adj_in = [cp(adj.at[0], adj.at[d], p.along(-d)) for d in range(1, 7)]
    par_in = [cp(par.at[0], par.at[d], p.along(-d)) for d in range(1, 5)]
    parb_in = [cp(par.at[0], parb.at[d - 1], p.along(d)) for d in (1, 2)]

    lax.fori_loop(6, DAYS, forward, 0)
    last = jnp.dot(W[1024:1040], x[DAYS], preferred_element_type=f32)
    rd[DAYS : DAYS + 1] = jnp.sum(last, axis=0, keepdims=True)
    readout = rd[1 : DAYS + 1]

    runoff = jnp.maximum(readout, 0.0) + jnp.log1p(jnp.exp(-jnp.abs(readout)))
    fS[0] = convolve(uh, runoff, pad)

    def send_flow(n):
        return [cp(fS.at[n], fR.at[n, d - 1], p.along(d)) for d in (1, 2)]

    flow_in = send_flow(0)

    for copy in par_in + adj_in:
        copy.wait_recv()
    level = [adj[d] for d in range(7)]
    kernels = [uh] + [hydro(par[d, 0:1], par[d, 1:2]) for d in range(1, 5)]
    indices = [index] + [par[d, 2:3].astype(jnp.int32) for d in range(1, 5)]
    start = level
    for count in (5, 3, 1):
        level = [
            start[j] + correlate(kernels[j], gather(level[j : j + 3], indices[j]), pad)
            for j in range(count)
        ]
    grad_runoff = level[0]
    grad_read = (0.5 * jnp.tanh(0.5 * readout) + 0.5) * grad_runoff
    grd[0:8] = jnp.zeros((8, REACH), f32)
    grd[8:24] = grad_read

    for copy in parb_in:
        copy.wait_recv()
    target = lax.broadcasted_iota(jnp.int32, (REACH, REACH), 0)
    for j in range(3):
        source = index if j == 0 else parb[j - 1, 2:3].astype(jnp.int32)
        route[j] = jnp.where(target == source - j * REACH, 1.0, 0.0).astype(bf16)

    def inflow(n):
        total = jnp.zeros((DAYS, REACH), f32)
        for j in range(3):
            flow = fS[n] if j == 0 else fR[n, j - 1]
            parts = jnp.concatenate(split3(flow), 0).astype(bf16)
            moved = lax.dot_general(parts, route[j], NT, preferred_element_type=f32)
            total = total + moved[0:16] + moved[16:32] + moved[32:48]
        return total

    accA[...] = jnp.zeros_like(accA)
    accB[...] = jnp.zeros_like(accB)
    gh[...] = jnp.zeros_like(gh)
    gcn[...] = jnp.zeros_like(gcn)

    def elementwise(t):
        gr = grd[pl.ds(t + 8, 1)]
        for c in range(0, HID, CHUNK):
            s = pl.ds(c, CHUNK)
            w = jnp.concatenate([wcol[s], wcol[s]], 1)
            ti = gates[0, t, s]
            tf = gates[1, t, s]
            tg = gates[2, t, s]
            to = gates[3, t, s]
            tc = jnp.tanh(cells[t + 1, s])
            ghw = (w * gr + gh[s]) * (1.0 + to)
            gc = ghw * (1.0 - tc * tc) + gcn[s]
            gci = gc * (1.0 + ti)
            gcf = gc * (1.0 + tf)
            gz[c : c + CHUNK] = (gci * ((1.0 - ti) * tg)).astype(bf16)
            gz[HID + c : HID + c + CHUNK] = (gcf * ((1.0 - tf) * cells[t, s])).astype(bf16)
            gz[2 * HID + c : 2 * HID + c + CHUNK] = (gci * (1.0 - tg * tg)).astype(bf16)
            gz[3 * HID + c : 3 * HID + c + CHUNK] = (ghw * ((1.0 - to) * tc)).astype(bf16)
            gcn[s] = gcf * 0.5

    def read_rows(row):
        hi, mid, _ = split3(row)
        return jnp.where(row16 == 0, hi, jnp.where(row16 == 1, mid, 0.0)).astype(bf16)

    def inputs_grad(t):
        small = lax.dot_general(
            x[t, 256:304], gz[0:1024], NT, preferred_element_type=f32
        )
        for j in range(8):
            accB[0, j] += small[0:24, j * 128 : (j + 1) * 128]
            accB[1, j] += small[24:48, j * 128 : (j + 1) * 128]

    def backward(i, _):
        t = DAYS - 1 - i
        elementwise(t)
        gh[...] = jnp.dot(WT[...], gz[0:1024], preferred_element_type=f32)
        gz[1024:1040] = read_rows(grd[pl.ds(t + 7, 1)])
        accA[...] += lax.dot_general(gz[...], x[t, 0:256], NT, preferred_element_type=f32)
        inputs_grad(t)
        return 0

    lax.fori_loop(0, 5, backward, 0)
    for n in (0, 1):
        for copy in flow_in:
            copy.wait_recv()
        fS[n + 1] = convolve(uh, runoff + inflow(n), pad)
        flow_in = send_flow(n + 1)
        lax.fori_loop(5 + 5 * n, 10 + 5 * n, backward, 0)

    own = p.r * 512
    other = (1 - p.r) * 512
    core = p.core()
    core_in = [
        cp(accA.at[rows(other + c * 256, 256)], bufA.at[pl.ds(c * 256, 256)], core)
        for c in range(2)
    ]
    elementwise(0)
    inputs_grad(0)
    last = lax.dot_general(
        read_rows(grd[DAYS + 7 : DAYS + 8]), x[DAYS, 0:256], NT, preferred_element_type=f32
    )
    out_row = jnp.sum(last + accA[1024:1040], axis=0, keepdims=True)
    for j in range(2):
        accB[1, j, 11:12] = out_row[:, j * 128 : (j + 1) * 128]
    core_b = cp(accB.at[1 - p.r], bufB, core)

    plane_in = []
    for c in range(2):
        core_in[c].wait_recv()
        for k in range(0, 256, 64):
            accA[rows(own + c * 256 + k, 64)] += bufA[c * 256 + k : c * 256 + k + 64]
        batch = []
        for d in range(1, 16):
            device, q = p.plane(d)
            batch.append(cp(accA.at[rows(own + c * 256 + q * 16, 16)], rsA.at[c, d - 1], device))
        plane_in.append(batch)
    core_b.wait_recv()
    accB[p.r] += bufB[...]
    line_b = []
    for d in range(1, 8):
        device, z = p.line(d)
        line_b.append(cp(accB.at[p.r, z], zB.at[d - 1], device))

    for copy in flow_in:
        copy.wait_recv()
    o_flow[...] = convolve(uh, runoff + inflow(2), pad)

    line_in = []
    for c in range(2):
        total = accA[rows(own + c * 256 + p.q * 16, 16)]
        for d in range(1, 16):
            plane_in[c][d - 1].wait_recv()
            total = total + rsA[c, d - 1]
        zA[c, p.z] = total
        mine = zA.at[c, p.z]
        line_in.append([cp(mine, mine, p.line(d)[0]) for d in range(1, 8)])
    total = accB[p.r, p.z]
    for d in range(1, 8):
        line_b[d - 1].wait_recv()
        total = total + zB[d - 1]
    xyB[p.q] = total
    mine = xyB.at[p.q]
    plane_b = [cp(mine, mine, p.plane(d)[0]) for d in range(1, 16)]

    factor = jnp.where(p.r == 0, 0.0625, 0.125).astype(f32)
    gathered = []
    passed = []
    for c in range(2):
        for copy in line_in[c]:
            copy.wait_recv()
        total = zA[c, 0]
        for z in range(1, 8):
            total = total + zA[c, z]
        mine = o_rec.at[rows(own + c * 256 + p.q * 16, 16)]
        mine[...] = total * factor
        gathered.append([cp(mine, mine, p.plane(d)[0]) for d in range(1, 16)])
        passed.append(cp(mine, mine, core))
    for copy in plane_b:
        copy.wait_recv()
    total = xyB[0]
    for q in range(1, 16):
        total = total + xyB[q]
    outB[p.r, p.z] = total
    mine = outB.at[p.r, p.z]
    gathered_b = [cp(mine, mine, p.line(d)[0]) for d in range(1, 8)]
    passed.append(cp(mine, mine, core))
    for c in range(2):
        for d in range(1, 16):
            gathered[c][d - 1].wait_recv()
            piece = o_rec.at[rows(own + c * 256 + p.plane_from(d) * 16, 16)]
            passed.append(cp(piece, piece, core))
    for d in range(1, 8):
        gathered_b[d - 1].wait_recv()
        piece = outB.at[p.r, p.line_from(d)]
        passed.append(cp(piece, piece, core))
    for copy in passed:
        copy.wait_recv()

    for j in range(8):
        s = slice(j * 128, (j + 1) * 128)
        back = 0.25 if j >= 4 else 0.125
        o_in[0:24, s] = outB[0, j] * back
        o_in[24:32, s] = outB[1, j, 0:8] * back
        o_bias[:, s] = outB[1, j, 8:9] * back
        if j < 2:
            o_out[:, s] = outB[1, j, 11:12] * 0.5
    cp.drain()


def per_device(
    forcing, w_in, w_rec, bias, w_out, uh_shape, uh_scale, reach_tier, reach_dest, out_cot
):
    vmem = pl.BlockSpec(memory_space=VMEM)
    flow, g_in, g_rec, g_bias, g_out = pl.pallas_call(
        kernel,
        out_shape=[
            jax.ShapeDtypeStruct((DAYS, REACH), f32),
            jax.ShapeDtypeStruct((FEAT, 1024), f32),
            jax.ShapeDtypeStruct((1024, HID), f32),
            jax.ShapeDtypeStruct((1, 1024), f32),
            jax.ShapeDtypeStruct((1, HID), f32),
        ],
        in_specs=[vmem] * 9,
        out_specs=[vmem] * 5,
        scratch_shapes=[
            VMEM((GROWS, XROWS), bf16),
            VMEM((HID, 1024), bf16),
            VMEM((HID, 128), f32),
            VMEM((DAYS + 1, XROWS, REACH), bf16),
            VMEM((4, DAYS, HID, REACH), f32),
            VMEM((DAYS + 1, HID, REACH), f32),
            VMEM((GROWS, REACH), bf16),
            VMEM((HID, REACH), f32),
            VMEM((HID, REACH), f32),
            VMEM((24, REACH), f32),
            VMEM((24, REACH), f32),
            VMEM((GROWS, HID), f32),
            VMEM((2, 8, 24, 128), f32),
            VMEM((32, REACH), f32),
            VMEM((7, DAYS, REACH), f32),
            VMEM((5, 8, REACH), f32),
            VMEM((2, 8, REACH), f32),
            VMEM((3, REACH, REACH), bf16),
            VMEM((3, DAYS, REACH), f32),
            VMEM((3, 2, DAYS, REACH), f32),
            VMEM((512, HID), f32),
            VMEM((2, 15, 16, HID), f32),
            VMEM((2, 8, 16, HID), f32),
            VMEM((8, 24, 128), f32),
            VMEM((7, 24, 128), f32),
            VMEM((16, 24, 128), f32),
            VMEM((2, 8, 24, 128), f32),
            pltpu.SemaphoreType.DMA((SEMS,)),
            pltpu.SemaphoreType.DMA((SEMS,)),
        ],
        compiler_params=pltpu.CompilerParams(
            collective_id=0, has_side_effects=True, vmem_limit_bytes=50 * 2**20
        ),
        name="river",
    )(
        forcing,
        w_in.T,
        w_rec,
        bias.reshape(1, 1024),
        w_out.reshape(1, HID),
        uh_shape.reshape(1, REACH),
        uh_scale.reshape(1, REACH),
        reach_dest.reshape(1, REACH),
        out_cot,
    )
    return (flow, g_in.T, g_rec, g_bias.reshape(1024), g_out.reshape(HID))


def solution(mesh):
    placed = (
        P(None, None, ("basin", "rep")),
        P(),
        P(),
        P(),
        P(),
        P(("basin", "rep")),
        P(("basin", "rep")),
        P(("basin", "rep")),
        P(("basin", "rep")),
        P(None, ("basin", "rep")),
    )
    return jax.shard_map(
        per_device,
        mesh=mesh,
        in_specs=placed,
        out_specs=(P(None, ("basin", "rep")), P(), P(), P(), P()),
        check_vma=False,
    )
```

```python
import jax
import jax.numpy as jnp
from jax import lax
from jax.experimental import pallas as pl
from jax.experimental.pallas import tpu as pltpu
from jax.sharding import PartitionSpec as P

MESH = pl.DeviceIdType.MESH
VMEM = pltpu.VMEM
f32 = jnp.float32
bf16 = jnp.bfloat16
DAYS = 16
HID = 256
FEAT = 32
REACH = 256
UHLEN = 8
XROWS = 304
GROWS = 1040
CHUNK = 32
SEMS = 280
PARTS = 4
PROWS = 512 // PARTS
OWNED = PROWS // 16
NT = (((1,), (1,)), ((), ()))


class Place:
    def __init__(self):
        self.b = lax.axis_index("basin")
        self.r = lax.axis_index("rep")
        self.x = self.b // 32
        self.y = (self.b // 8) % 4
        self.z = self.b % 8
        self.q = self.x * 4 + self.y

    def core(self):
        return (self.b, 1 - self.r)

    def plane(self, d):
        px = lax.rem(self.x + d // 4, 4)
        py = lax.rem(self.y + d % 4, 4)
        return (px * 32 + py * 8 + self.z, self.r), px * 4 + py

    def plane_from(self, d):
        return lax.rem(self.x + 4 - d // 4, 4) * 4 + lax.rem(self.y + 4 - d % 4, 4)

    def line(self, d):
        pz = lax.rem(self.z + d, 8)
        return (self.x * 32 + self.y * 8 + pz, self.r), pz

    def line_from(self, d):
        return lax.rem(self.z + 8 - d, 8)

    def along(self, d):
        return (lax.rem(self.b + 128 + d, 128), self.r)


class Copies:
    def __init__(self, send, recv):
        self.send = send
        self.recv = recv
        self.all = []

    def __call__(self, src, dst, device):
        i = len(self.all)
        copy = pltpu.make_async_remote_copy(
            src_ref=src,
            dst_ref=dst,
            send_sem=self.send.at[i],
            recv_sem=self.recv.at[i],
            device_id=device,
            device_id_type=MESH,
        )
        copy.start()
        self.all.append(copy)
        return copy

    def drain(self):
        for copy in self.all:
            copy.wait_send()


def rows(start, size):
    return pl.ds(pl.multiple_of(start, 8), size)


def split3(v):
    hi = v.astype(bf16).astype(f32)
    mid = (v - hi).astype(bf16).astype(f32)
    return hi, mid, v - hi - mid


def hydro(shape_row, scale_row):
    lag = lax.broadcasted_iota(jnp.int32, (UHLEN, REACH), 0).astype(f32) + 1.0
    u = jnp.exp((shape_row - 1.0) * jnp.log(lag) - lag / scale_row)
    return u / jnp.sum(u, axis=0, keepdims=True)


def convolve(uh, series, pad):
    pad[8:24] = series
    total = uh[0:1] * series
    for m in range(1, UHLEN):
        total = total + uh[m : m + 1] * pad[8 - m : 24 - m]
    return total


def correlate(uh, series, pad):
    pad[8:24] = series
    total = uh[0:1] * series
    for m in range(1, UHLEN):
        total = total + uh[m : m + 1] * pad[8 + m : 24 + m]
    return total


def gather(blocks, index):
    halves = []
    for h in range(2):
        idx = jnp.broadcast_to(index[:, h * 128 : (h + 1) * 128], (DAYS, 128))
        lane = jnp.bitwise_and(idx, 127)
        block = jnp.right_shift(idx, 7)
        total = jnp.zeros((DAYS, 128), f32)
        for i in range(6):
            source = blocks[i // 2][:, (i % 2) * 128 : (i % 2 + 1) * 128]
            picked = jnp.take_along_axis(source, lane, axis=1)
            total = jnp.where(block == i, picked, total)
        halves.append(total)
    return jnp.concatenate(halves, 1)


def kernel(
    forcing_h, w_in_t_h, w_rec_h, bias_h, w_out_h, uh_shape_h, uh_scale_h, dest_h, cot_h,
    o_flow, o_in, o_rec, o_bias, o_out,
    w_in_t, w_rec, bias, w_out, uh_shape, uh_scale, dest, cot, load_sem,
    W, WT, wcol, x, fac, cells, gz, gh, gcn, rd, grd,
    accA, accB, pad, adj, par, parb, route, fS, fR,
    bufA, rsA, zA, bufB, zB, xyB, outB, send, recv,
):
    p = Place()
    cp = Copies(send, recv)

    loads = [
        pltpu.make_async_copy(src, dst, load_sem.at[i])
        for i, (src, dst) in enumerate((
            (uh_shape_h, uh_shape), (uh_scale_h, uh_scale), (dest_h, dest), (cot_h, cot),
            (w_rec_h, w_rec), (w_in_t_h, w_in_t), (bias_h, bias), (w_out_h, w_out),
            (forcing_h, x.at[0:DAYS, 256:288]),
        ))
    ]
    for load in loads:
        load.start()

    barrier = pltpu.get_barrier_semaphore()
    partners = [p.core()]
    partners += [p.plane(d)[0] for d in range(1, 16)]
    partners += [p.line(d)[0] for d in range(1, 8)]
    partners += [p.along(d) for d in (1, 2, 3, 4, 5, 6, -1, -2, -3, -4, -5, -6)]
    for device in partners:
        pl.semaphore_signal(barrier, inc=1, device_id=device, device_id_type=MESH)

    pad[...] = jnp.zeros_like(pad)
    for load in loads[0:4]:
        load.wait()
    uh = hydro(uh_shape[...], uh_scale[...])
    dest_row = dest[...]
    linked = dest_row >= 0
    ahead = jnp.right_shift(dest_row, 9) - p.b
    index = jnp.where(linked, ahead * REACH + jnp.bitwise_and(dest_row, REACH - 1), -1)
    row8 = lax.broadcasted_iota(jnp.int32, (8, REACH), 0)
    par[0] = jnp.where(
        row8 == 0, uh_shape[...], jnp.where(row8 == 1, uh_scale[...], index.astype(f32))
    )
    adj[0] = correlate(uh, cot[...], pad)

    for load in loads[4:]:
        load.wait()

    for k in range(0, 1024, 128):
        half = 0.5 if k // 256 == 2 else 0.25
        back = 0.25 if k // 256 >= 2 else 0.125
        block = w_rec[k : k + 128].astype(f32)
        W[k : k + 128, 0:256] = (block * half).astype(bf16)
        WT[:, k : k + 128] = (block.T * back).astype(bf16)
        part = w_in_t[:, k : k + 128].astype(f32) * (2.0 * half)
        hi, mid, lo = split3(bias[:, k : k + 128] * (2.0 * half))
        row = lax.broadcasted_iota(jnp.int32, (96, 128), 0)
        rest = jnp.where(row == 0, hi, jnp.where(row == 1, mid, jnp.where(row == 2, lo, 0.0)))
        W[k : k + 128, 256:304] = jnp.concatenate([part, rest], 0).T[:, 0:48].astype(bf16)
    row16 = lax.broadcasted_iota(jnp.int32, (16, REACH), 0)
    hi, mid, lo = split3(w_out[...] * 0.5)
    W[1024:1040, 0:256] = jnp.where(
        row16 == 0, hi, jnp.where(row16 == 1, mid, jnp.where(row16 == 2, lo, 0.0))
    ).astype(bf16)
    W[1024:1040, 256:304] = jnp.zeros((16, 48), bf16)
    wcol[...] = jnp.broadcast_to(w_out[...], (128, HID)).T

    x[0, 0:256] = jnp.zeros((HID, REACH), bf16)
    ones = jnp.where(row16 < 3, 1.0, 0.0).astype(bf16)
    for t in range(DAYS):
        x[t, 288:304] = ones
    x[DAYS, 256:304] = jnp.zeros((48, REACH), bf16)
    cells[...] = jnp.zeros((HID, REACH), f32)

    def forward(t, _):
        pre = jnp.dot(W[...], x[t], preferred_element_type=f32)
        rd[pl.ds(t, 1)] = jnp.sum(pre[1024:1032], axis=0, keepdims=True)
        for c in range(0, HID, CHUNK):
            s = pl.ds(c, CHUNK)
            ti = jnp.tanh(pre[c : c + CHUNK])
            tf = jnp.tanh(pre[HID + c : HID + c + CHUNK])
            tg = jnp.tanh(pre[2 * HID + c : 2 * HID + c + CHUNK])
            to = jnp.tanh(pre[3 * HID + c : 3 * HID + c + CHUNK])
            i1 = 1.0 + ti
            f1 = 1.0 + tf
            o1 = 1.0 + to
            before = cells[s]
            cell = 0.5 * (f1 * before + i1 * tg)
            tc = jnp.tanh(cell)
            h2 = o1 * tc
            fac[0, t, s] = i1 * ((1.0 - ti) * tg)
            fac[1, t, s] = f1 * ((1.0 - tf) * before)
            fac[2, t, s] = i1 * (1.0 - tg * tg)
            fac[3, t, s] = h2 * (1.0 - to)
            fac[4, t, s] = o1 * (1.0 - tc * tc)
            fac[5, t, s] = 0.5 * f1
            cells[s] = cell
            x[t + 1, s] = h2.astype(bf16)
        return 0

    pl.semaphore_wait(barrier, len(partners))
    par_in = [cp(par.at[0], par.at[d], p.along(-d)) for d in range(4, 0, -1)]
    adj_in = [cp(adj.at[0], adj.at[d], p.along(-d)) for d in range(6, 0, -1)]
    parb_in = [cp(par.at[0], parb.at[d - 1], p.along(d)) for d in (1, 2)]

    lax.fori_loop(0, DAYS, forward, 0)
    last = jnp.dot(W[1024:1040], x[DAYS], preferred_element_type=f32)
    rd[DAYS : DAYS + 1] = jnp.sum(last, axis=0, keepdims=True)
    readout = rd[1 : DAYS + 1]

    runoff = jnp.maximum(readout, 0.0) + jnp.log1p(jnp.exp(-jnp.abs(readout)))
    fS[0] = convolve(uh, runoff, pad)

    def send_flow(n):
        return [cp(fS.at[n], fR.at[n, d - 1], p.along(d)) for d in (1, 2)]

    flow_in = send_flow(0)

    for copy in par_in + adj_in:
        copy.wait_recv()
    level = [adj[d] for d in range(7)]
    kernels = [uh] + [hydro(par[d, 0:1], par[d, 1:2]) for d in range(1, 5)]
    indices = [index] + [par[d, 2:3].astype(jnp.int32) for d in range(1, 5)]
    start = level
    for count in (5, 3, 1):
        level = [
            start[j] + correlate(kernels[j], gather(level[j : j + 3], indices[j]), pad)
            for j in range(count)
        ]
    grad_runoff = level[0]
    grad_read = (0.5 * jnp.tanh(0.5 * readout) + 0.5) * grad_runoff
    grd[0:8] = jnp.zeros((8, REACH), f32)
    grd[8:24] = grad_read

    for copy in parb_in:
        copy.wait_recv()
    target = lax.broadcasted_iota(jnp.int32, (REACH, REACH), 0)
    for j in range(3):
        source = index if j == 0 else parb[j - 1, 2:3].astype(jnp.int32)
        route[j] = jnp.where(target == source - j * REACH, 1.0, 0.0).astype(bf16)

    def inflow(n):
        total = jnp.zeros((DAYS, REACH), f32)
        for j in range(3):
            flow = fS[n] if j == 0 else fR[n, j - 1]
            parts = jnp.concatenate(split3(flow), 0).astype(bf16)
            moved = lax.dot_general(parts, route[j], NT, preferred_element_type=f32)
            total = total + moved[0:16] + moved[16:32] + moved[32:48]
        return total

    accB[...] = jnp.zeros_like(accB)

    def elementwise(t):
        gr = grd[t + 8 : t + 9]
        for c in range(0, HID, CHUNK):
            s = pl.ds(c, CHUNK)
            ghc = jnp.concatenate([wcol[s], wcol[s]], 1) * gr
            if t < DAYS - 1:
                ghc = ghc + gh[s]
            gc = ghc * fac[4, t, s]
            if t < DAYS - 1:
                gc = gc + gcn[s]
            gz[c : c + CHUNK] = (gc * fac[0, t, s]).astype(bf16)
            gz[HID + c : HID + c + CHUNK] = (gc * fac[1, t, s]).astype(bf16)
            gz[2 * HID + c : 2 * HID + c + CHUNK] = (gc * fac[2, t, s]).astype(bf16)
            gz[3 * HID + c : 3 * HID + c + CHUNK] = (ghc * fac[3, t, s]).astype(bf16)
            gcn[s] = gc * fac[5, t, s]

    def read_rows(row):
        hi, mid, _ = split3(row)
        return jnp.where(row16 == 0, hi, jnp.where(row16 == 1, mid, 0.0)).astype(bf16)

    def inputs_grad(t):
        small = lax.dot_general(
            x[t, 256:304], gz[0:1024], NT, preferred_element_type=f32
        )
        for j in range(8):
            accB[0, j] += small[0:24, j * 128 : (j + 1) * 128]
            accB[1, j] += small[24:48, j * 128 : (j + 1) * 128]

    def carry(t):
        gh[...] = jnp.dot(WT[...], gz[0:1024], preferred_element_type=f32)

    def rec_grad(t, s):
        term = lax.dot_general(gz[s], x[t, 0:256], NT, preferred_element_type=f32)
        accA[s] = term if t == DAYS - 1 else accA[s] + term

    own = p.r * 512
    other = (1 - p.r) * 512
    core = p.core()
    for t in range(DAYS - 1, 0, -1):
        elementwise(t)
        gz[1024:1040] = read_rows(grd[t + 7 : t + 8])
        if t > 1:
            carry(t)
            rec_grad(t, slice(0, GROWS))
        else:
            rec_grad(t, rows(other, 512))
            core_in = [
                cp(
                    accA.at[rows(other + c * PROWS, PROWS)],
                    bufA.at[pl.ds(c * PROWS, PROWS)],
                    core,
                )
                for c in range(PARTS)
            ]
            carry(t)
            rec_grad(t, rows(own, 512))
            rec_grad(t, slice(1024, GROWS))
        inputs_grad(t)
        if t in (11, 6):
            n = 0 if t == 11 else 1
            for copy in flow_in:
                copy.wait_recv()
            fS[n + 1] = convolve(uh, runoff + inflow(n), pad)
            flow_in = send_flow(n + 1)

    elementwise(0)
    inputs_grad(0)
    last = lax.dot_general(
        read_rows(grd[DAYS + 7 : DAYS + 8]), x[DAYS, 0:256], NT, preferred_element_type=f32
    )
    out_row = jnp.sum(last + accA[1024:1040], axis=0, keepdims=True)
    for j in range(2):
        accB[1, j, 11:12] = out_row[:, j * 128 : (j + 1) * 128]
    core_b = cp(accB.at[1 - p.r], bufB, core)

    plane_in = []
    for c in range(PARTS):
        core_in[c].wait_recv()
        for k in range(0, PROWS, 64):
            accA[rows(own + c * PROWS + k, 64)] += bufA[c * PROWS + k : c * PROWS + k + 64]
        batch = []
        for d in range(1, 16):
            device, q = p.plane(d)
            part = accA.at[rows(own + c * PROWS + q * OWNED, OWNED)]
            batch.append(cp(part, rsA.at[c, d - 1], device))
        plane_in.append(batch)
    core_b.wait_recv()
    accB[p.r] += bufB[...]
    line_b = []
    for d in range(1, 8):
        device, z = p.line(d)
        line_b.append(cp(accB.at[p.r, z], zB.at[d - 1], device))

    for copy in flow_in:
        copy.wait_recv()
    o_flow[...] = convolve(uh, runoff + inflow(2), pad)

    line_in = []
    for c in range(PARTS):
        total = accA[rows(own + c * PROWS + p.q * OWNED, OWNED)]
        for d in range(1, 16):
            plane_in[c][d - 1].wait_recv()
            total = total + rsA[c, d - 1]
        zA[c, p.z] = total
        mine = zA.at[c, p.z]
        line_in.append([cp(mine, mine, p.line(d)[0]) for d in range(1, 8)])
    total = accB[p.r, p.z]
    for d in range(1, 8):
        line_b[d - 1].wait_recv()
        total = total + zB[d - 1]
    xyB[p.q] = total
    mine = xyB.at[p.q]
    plane_b = [cp(mine, mine, p.plane(d)[0]) for d in range(1, 16)]

    factor = jnp.where(p.r == 0, 0.0625, 0.125).astype(f32)
    gathered = []
    passed = []
    for c in range(PARTS):
        for copy in line_in[c]:
            copy.wait_recv()
        total = zA[c, 0]
        for z in range(1, 8):
            total = total + zA[c, z]
        mine = o_rec.at[rows(own + c * PROWS + p.q * OWNED, OWNED)]
        mine[...] = total * factor
        gathered.append([cp(mine, mine, p.plane(d)[0]) for d in range(1, 16)])
        passed.append(cp(mine, mine, core))
    for copy in plane_b:
        copy.wait_recv()
    total = xyB[0]
    for q in range(1, 16):
        total = total + xyB[q]
    outB[p.r, p.z] = total
    mine = outB.at[p.r, p.z]
    gathered_b = [cp(mine, mine, p.line(d)[0]) for d in range(1, 8)]
    passed.append(cp(mine, mine, core))
    for c in range(PARTS):
        for d in range(1, 16):
            gathered[c][d - 1].wait_recv()
            piece = o_rec.at[rows(own + c * PROWS + p.plane_from(d) * OWNED, OWNED)]
            passed.append(cp(piece, piece, core))
    for d in range(1, 8):
        gathered_b[d - 1].wait_recv()
        piece = outB.at[p.r, p.line_from(d)]
        passed.append(cp(piece, piece, core))
    for copy in passed:
        copy.wait_recv()

    for j in range(8):
        s = slice(j * 128, (j + 1) * 128)
        back = 0.25 if j >= 4 else 0.125
        o_in[0:24, s] = outB[0, j] * back
        o_in[24:32, s] = outB[1, j, 0:8] * back
        o_bias[:, s] = outB[1, j, 8:9] * back
        if j < 2:
            o_out[:, s] = outB[1, j, 11:12] * 0.5
    cp.drain()


def write_out(*refs):
    copies = [
        pltpu.make_async_copy(refs[i], refs[5 + i], refs[10].at[i]) for i in range(5)
    ]
    for copy in copies:
        copy.start()
    for copy in copies:
        copy.wait()


def per_device(
    forcing, w_in, w_rec, bias, w_out, uh_shape, uh_scale, reach_tier, reach_dest, out_cot
):
    vmem = pl.BlockSpec(memory_space=VMEM)
    results = [
        jax.ShapeDtypeStruct((DAYS, REACH), f32),
        jax.ShapeDtypeStruct((FEAT, 1024), f32),
        jax.ShapeDtypeStruct((1024, HID), f32),
        jax.ShapeDtypeStruct((1, 1024), f32),
        jax.ShapeDtypeStruct((1, HID), f32),
    ]
    held = pl.pallas_call(
        kernel,
        out_shape=results,
        in_specs=[pl.BlockSpec(memory_space=pltpu.HBM)] * 9,
        out_specs=[vmem] * 5,
        scratch_shapes=[
            VMEM((FEAT, 1024), bf16),
            VMEM((1024, HID), bf16),
            VMEM((1, 1024), f32),
            VMEM((1, HID), f32),
            VMEM((1, REACH), f32),
            VMEM((1, REACH), f32),
            VMEM((1, REACH), jnp.int32),
            VMEM((DAYS, REACH), f32),
            pltpu.SemaphoreType.DMA((9,)),
            VMEM((GROWS, XROWS), bf16),
            VMEM((HID, 1024), bf16),
            VMEM((HID, 128), f32),
            VMEM((DAYS + 1, XROWS, REACH), bf16),
            VMEM((6, DAYS, HID, REACH), f32),
            VMEM((HID, REACH), f32),
            VMEM((GROWS, REACH), bf16),
            VMEM((HID, REACH), f32),
            VMEM((HID, REACH), f32),
            VMEM((24, REACH), f32),
            VMEM((24, REACH), f32),
            VMEM((GROWS, HID), f32),
            VMEM((2, 8, 24, 128), f32),
            VMEM((32, REACH), f32),
            VMEM((7, DAYS, REACH), f32),
            VMEM((5, 8, REACH), f32),
            VMEM((2, 8, REACH), f32),
            VMEM((3, REACH, REACH), bf16),
            VMEM((3, DAYS, REACH), f32),
            VMEM((3, 2, DAYS, REACH), f32),
            VMEM((512, HID), f32),
            VMEM((PARTS, 15, OWNED, HID), f32),
            VMEM((PARTS, 8, OWNED, HID), f32),
            VMEM((8, 24, 128), f32),
            VMEM((7, 24, 128), f32),
            VMEM((16, 24, 128), f32),
            VMEM((2, 8, 24, 128), f32),
            pltpu.SemaphoreType.DMA((SEMS,)),
            pltpu.SemaphoreType.DMA((SEMS,)),
        ],
        compiler_params=pltpu.CompilerParams(
            collective_id=0, has_side_effects=True, vmem_limit_bytes=50 * 2**20
        ),
        name="river",
    )(
        *(
            pltpu.with_memory_space_constraint(operand, pltpu.HBM)
            for operand in (
                forcing,
                w_in.T,
                w_rec,
                bias.reshape(1, 1024),
                w_out.reshape(1, HID),
                uh_shape.reshape(1, REACH),
                uh_scale.reshape(1, REACH),
                reach_dest.reshape(1, REACH),
                out_cot,
            )
        )
    )
    flow, g_in, g_rec, g_bias, g_out = pl.pallas_call(
        write_out,
        out_shape=results,
        in_specs=[vmem] * 5,
        out_specs=[pl.BlockSpec(memory_space=pltpu.HBM)] * 5,
        scratch_shapes=[pltpu.SemaphoreType.DMA((5,))],
        name="write_out",
    )(*held)
    return (flow, g_in.T, g_rec, g_bias.reshape(1024), g_out.reshape(HID))


def solution(mesh):
    placed = (
        P(None, None, ("basin", "rep")),
        P(),
        P(),
        P(),
        P(),
        P(("basin", "rep")),
        P(("basin", "rep")),
        P(("basin", "rep")),
        P(("basin", "rep")),
        P(None, ("basin", "rep")),
    )
    return jax.shard_map(
        per_device,
        mesh=mesh,
        in_specs=placed,
        out_specs=(P(None, ("basin", "rep")), P(), P(), P(), P()),
        check_vma=False,
    )
```

```python
import jax
import jax.numpy as jnp
from jax import lax
from jax.experimental import pallas as pl
from jax.experimental.pallas import tpu as pltpu
from jax.sharding import PartitionSpec as P

MESH = pl.DeviceIdType.MESH
VMEM = pltpu.VMEM
f32 = jnp.float32
bf16 = jnp.bfloat16
DAYS = 16
HID = 256
FEAT = 32
REACH = 256
UHLEN = 8
XROWS = 304
GROWS = 1040
CHUNK = 32
SEMS = 64
PARTS = 4
PROWS = 512 // PARTS
OWNED = PROWS // 16
NT = (((1,), (1,)), ((), ()))


class Place:
    def __init__(self):
        self.b = lax.axis_index("basin")
        self.r = lax.axis_index("rep")
        self.x = self.b // 32
        self.y = (self.b // 8) % 4
        self.z = self.b % 8
        self.q = self.x * 4 + self.y

    def core(self):
        return (self.b, 1 - self.r)

    def plane(self, d):
        px = lax.rem(self.x + d // 4, 4)
        py = lax.rem(self.y + d % 4, 4)
        return (px * 32 + py * 8 + self.z, self.r), px * 4 + py

    def plane_from(self, d):
        return lax.rem(self.x + 4 - d // 4, 4) * 4 + lax.rem(self.y + 4 - d % 4, 4)

    def line(self, d):
        pz = lax.rem(self.z + d, 8)
        return (self.x * 32 + self.y * 8 + pz, self.r), pz

    def line_from(self, d):
        return lax.rem(self.z + 8 - d, 8)

    def along(self, d):
        return (lax.rem(self.b + 128 + d, 128), self.r)


class Copies:
    def __init__(self, send, recv):
        self.send = send
        self.recv = recv
        self.all = []

    def describe(self, i, src, dst, device):
        return pltpu.make_async_remote_copy(
            src_ref=src,
            dst_ref=dst,
            send_sem=self.send.at[i],
            recv_sem=self.recv.at[i],
            device_id=device,
            device_id_type=MESH,
        )

    def __call__(self, src, dst, device):
        return self.many([(src, dst, device)], src)

    def many(self, copies, whole):
        i = len(self.all)
        for src, dst, device in copies:
            self.describe(i, src, dst, device).start()
        self.all.append(self.describe(i, whole, whole, copies[0][2]))
        return self.all[-1]

    def drain(self):
        for copy in self.all:
            copy.wait_send()


PLANE = sorted(range(1, 16), key=lambda d: (-min(d // 4, 4 - d // 4) - min(d % 4, 4 - d % 4), d))
LINE = (4, 3, 5, 2, 6, 1, 7)


def rows(start, size):
    return pl.ds(pl.multiple_of(start, 8), size)


def split3(v):
    hi = v.astype(bf16).astype(f32)
    mid = (v - hi).astype(bf16).astype(f32)
    return hi, mid, v - hi - mid


def hydro(shape_row, scale_row):
    lag = lax.broadcasted_iota(jnp.int32, (UHLEN, REACH), 0).astype(f32) + 1.0
    u = jnp.exp((shape_row - 1.0) * jnp.log(lag) - lag / scale_row)
    return u / jnp.sum(u, axis=0, keepdims=True)


def convolve(uh, series, pad):
    pad[8:24] = series
    total = uh[0:1] * series
    for m in range(1, UHLEN):
        total = total + uh[m : m + 1] * pad[8 - m : 24 - m]
    return total


def correlate(uh, series, pad):
    pad[8:24] = series
    total = uh[0:1] * series
    for m in range(1, UHLEN):
        total = total + uh[m : m + 1] * pad[8 + m : 24 + m]
    return total


def gather(blocks, index):
    halves = []
    for h in range(2):
        idx = jnp.broadcast_to(index[:, h * 128 : (h + 1) * 128], (DAYS, 128))
        lane = jnp.bitwise_and(idx, 127)
        block = jnp.right_shift(idx, 7)
        total = jnp.zeros((DAYS, 128), f32)
        for i in range(6):
            source = blocks[i // 2][:, (i % 2) * 128 : (i % 2 + 1) * 128]
            picked = jnp.take_along_axis(source, lane, axis=1)
            total = jnp.where(block == i, picked, total)
        halves.append(total)
    return jnp.concatenate(halves, 1)


def kernel(
    forcing_h, w_in_t_h, w_rec_h, bias_h, w_out_h, uh_shape_h, uh_scale_h, dest_h, cot_h,
    o_flow, o_in, o_rec, o_bias, o_out,
    w_in_t, w_rec, bias, w_out, uh_shape, uh_scale, dest, cot, load_sem,
    W, WT, wcol, x, fac, cells, gz, gh, gcn, rd, grd,
    accA, accB, pad, adj, route, fS, fR,
    bufA, rsA, zA, bufB, zB, xyB, outB, send, recv,
):
    p = Place()
    cp = Copies(send, recv)

    barrier = pltpu.get_barrier_semaphore()
    partners = [p.along(d) for d in (6, 5, 4, 3, 2, 1, -6, -5, -4, -3, -2, -1)]
    partners += [p.plane(d)[0] for d in PLANE]
    partners += [p.line(d)[0] for d in LINE]
    partners += [p.core()]
    for device in partners:
        pl.semaphore_signal(barrier, inc=1, device_id=device, device_id_type=MESH)

    loads = [
        pltpu.make_async_copy(src, dst, load_sem.at[i])
        for i, (src, dst) in enumerate((
            (uh_shape_h, uh_shape), (uh_scale_h, uh_scale), (dest_h, dest), (cot_h, cot),
            (w_rec_h, w_rec), (w_in_t_h, w_in_t), (bias_h, bias), (w_out_h, w_out),
            (forcing_h, x.at[0:DAYS, 256:288]),
        ))
    ]
    for load in loads:
        load.start()

    pad[...] = jnp.zeros_like(pad)
    for load in loads[0:4]:
        load.wait()
    uh = hydro(uh_shape[...], uh_scale[...])
    dest_row = dest[...]
    linked = dest_row >= 0
    ahead = jnp.right_shift(dest_row, 9) - p.b
    index = jnp.where(linked, ahead * REACH + jnp.bitwise_and(dest_row, REACH - 1), -1)
    adj[0, 0:16] = correlate(uh, cot[...], pad)
    row8 = lax.broadcasted_iota(jnp.int32, (8, REACH), 0)
    adj[0, 16:24] = jnp.where(
        row8 == 0, uh_shape[...], jnp.where(row8 == 1, uh_scale[...], index.astype(f32))
    )
    fS[0, 16:24] = jnp.broadcast_to(index.astype(f32), (8, REACH))

    for load in loads[4:]:
        load.wait()

    for k in range(0, 1024, 128):
        half = 0.5 if k // 256 == 2 else 0.25
        back = 0.25 if k // 256 >= 2 else 0.125
        block = w_rec[k : k + 128].astype(f32)
        W[k : k + 128, 0:256] = (block * half).astype(bf16)
        WT[:, k : k + 128] = (block.T * back).astype(bf16)
        part = w_in_t[:, k : k + 128].astype(f32) * (2.0 * half)
        hi, mid, lo = split3(bias[:, k : k + 128] * (2.0 * half))
        row = lax.broadcasted_iota(jnp.int32, (96, 128), 0)
        rest = jnp.where(row == 0, hi, jnp.where(row == 1, mid, jnp.where(row == 2, lo, 0.0)))
        W[k : k + 128, 256:304] = jnp.concatenate([part, rest], 0).T[:, 0:48].astype(bf16)
    row16 = lax.broadcasted_iota(jnp.int32, (16, REACH), 0)
    hi, mid, lo = split3(w_out[...] * 0.5)
    W[1024:1040, 0:256] = jnp.where(
        row16 == 0, hi, jnp.where(row16 == 1, mid, jnp.where(row16 == 2, lo, 0.0))
    ).astype(bf16)
    W[1024:1040, 256:304] = jnp.zeros((16, 48), bf16)
    wcol[...] = jnp.broadcast_to(w_out[...], (128, HID)).T

    x[0, 0:256] = jnp.zeros((HID, REACH), bf16)
    ones = jnp.where(row16 < 3, 1.0, 0.0).astype(bf16)
    for t in range(DAYS):
        x[t, 288:304] = ones
    x[DAYS, 256:304] = jnp.zeros((48, REACH), bf16)
    cells[...] = jnp.zeros((HID, REACH), f32)

    def forward(t, _):
        pre = jnp.dot(W[...], x[t], preferred_element_type=f32)
        rd[pl.ds(t, 1)] = jnp.sum(pre[1024:1032], axis=0, keepdims=True)
        for c in range(0, HID, CHUNK):
            s = pl.ds(c, CHUNK)
            ti = jnp.tanh(pre[c : c + CHUNK])
            tf = jnp.tanh(pre[HID + c : HID + c + CHUNK])
            tg = jnp.tanh(pre[2 * HID + c : 2 * HID + c + CHUNK])
            to = jnp.tanh(pre[3 * HID + c : 3 * HID + c + CHUNK])
            i1 = 1.0 + ti
            f1 = 1.0 + tf
            o1 = 1.0 + to
            before = cells[s]
            cell = 0.5 * (f1 * before + i1 * tg)
            tc = jnp.tanh(cell)
            h2 = o1 * tc
            fac[0, t, s] = i1 * ((1.0 - ti) * tg)
            fac[1, t, s] = f1 * ((1.0 - tf) * before)
            fac[2, t, s] = i1 * (1.0 - tg * tg)
            fac[3, t, s] = h2 * (1.0 - to)
            fac[4, t, s] = o1 * (1.0 - tc * tc)
            fac[5, t, s] = 0.5 * f1
            cells[s] = cell
            x[t + 1, s] = h2.astype(bf16)
        return 0

    pl.semaphore_wait(barrier, len(partners))
    adj_in = [
        cp(adj.at[0, 0 : 24 if d < 5 else 16], adj.at[d, 0 : 24 if d < 5 else 16], p.along(-d))
        for d in range(6, 0, -1)
    ]
    lax.fori_loop(0, DAYS, forward, 0)
    last = jnp.dot(W[1024:1040], x[DAYS], preferred_element_type=f32)
    rd[DAYS : DAYS + 1] = jnp.sum(last, axis=0, keepdims=True)
    readout = rd[1 : DAYS + 1]

    runoff = jnp.maximum(readout, 0.0) + jnp.log1p(jnp.exp(-jnp.abs(readout)))
    fS[0, 0:16] = convolve(uh, runoff, pad)

    def send_flow(n):
        size = 24 if n == 0 else 16
        return [cp(fS.at[n, 0:size], fR.at[n, d - 1, 0:size], p.along(d)) for d in (2, 1)]

    flow_in = send_flow(0)

    for copy in adj_in:
        copy.wait_recv()
    level = [adj[d, 0:16] for d in range(7)]
    kernels = [uh] + [hydro(adj[d, 16:17], adj[d, 17:18]) for d in range(1, 5)]
    indices = [index] + [adj[d, 18:19].astype(jnp.int32) for d in range(1, 5)]
    start = level
    for count in (5, 3, 1):
        level = [
            start[j] + correlate(kernels[j], gather(level[j : j + 3], indices[j]), pad)
            for j in range(count)
        ]
    grad_runoff = level[0]
    grad_read = (0.5 * jnp.tanh(0.5 * readout) + 0.5) * grad_runoff
    grd[0:8] = jnp.zeros((8, REACH), f32)
    grd[8:24] = grad_read

    def inflow(n):
        total = jnp.zeros((DAYS, REACH), f32)
        for j in range(3):
            flow = fS[n, 0:16] if j == 0 else fR[n, j - 1, 0:16]
            parts = jnp.concatenate(split3(flow), 0).astype(bf16)
            moved = lax.dot_general(parts, route[j], NT, preferred_element_type=f32)
            total = total + moved[0:16] + moved[16:32] + moved[32:48]
        return total

    accB[...] = jnp.zeros_like(accB)

    def elementwise(t):
        gr = grd[t + 8 : t + 9]
        for c in range(0, HID, CHUNK):
            s = pl.ds(c, CHUNK)
            ghc = jnp.concatenate([wcol[s], wcol[s]], 1) * gr
            if t < DAYS - 1:
                ghc = ghc + gh[s]
            gc = ghc * fac[4, t, s]
            if t < DAYS - 1:
                gc = gc + gcn[s]
            gz[c : c + CHUNK] = (gc * fac[0, t, s]).astype(bf16)
            gz[HID + c : HID + c + CHUNK] = (gc * fac[1, t, s]).astype(bf16)
            gz[2 * HID + c : 2 * HID + c + CHUNK] = (gc * fac[2, t, s]).astype(bf16)
            gz[3 * HID + c : 3 * HID + c + CHUNK] = (ghc * fac[3, t, s]).astype(bf16)
            gcn[s] = gc * fac[5, t, s]

    def read_rows(row):
        hi, mid, _ = split3(row)
        return jnp.where(row16 == 0, hi, jnp.where(row16 == 1, mid, 0.0)).astype(bf16)

    def inputs_grad(t):
        small = lax.dot_general(
            x[t, 256:304], gz[0:1024], NT, preferred_element_type=f32
        )
        for j in range(8):
            accB[0, j] += small[0:24, j * 128 : (j + 1) * 128]
            accB[1, j] += small[24:48, j * 128 : (j + 1) * 128]

    def carry(t):
        gh[...] = jnp.dot(WT[...], gz[0:1024], preferred_element_type=f32)

    def rec_grad(t, s):
        term = lax.dot_general(gz[s], x[t, 0:256], NT, preferred_element_type=f32)
        accA[s] = term if t == DAYS - 1 else accA[s] + term

    own = p.r * 512
    other = (1 - p.r) * 512
    core = p.core()
    for t in range(DAYS - 1, 0, -1):
        elementwise(t)
        gz[1024:1040] = read_rows(grd[t + 7 : t + 8])
        if t > 1:
            carry(t)
            rec_grad(t, slice(0, GROWS))
        else:
            rec_grad(t, rows(other, 512))
            core_in = [
                cp(
                    accA.at[rows(other + c * PROWS, PROWS)],
                    bufA.at[pl.ds(c * PROWS, PROWS)],
                    core,
                )
                for c in range(PARTS)
            ]
            carry(t)
            rec_grad(t, rows(own, 512))
            rec_grad(t, slice(1024, GROWS))
        inputs_grad(t)
        if t == 8:
            for copy in flow_in:
                copy.wait_recv()
            target = lax.broadcasted_iota(jnp.int32, (REACH, REACH), 0)
            for j in range(3):
                source = index if j == 0 else fR[0, j - 1, 16:17].astype(jnp.int32)
                route[j] = jnp.where(target == source - j * REACH, 1.0, 0.0).astype(bf16)
            fS[1, 0:16] = convolve(uh, runoff + inflow(0), pad)
            flow_in = send_flow(1)

    elementwise(0)
    inputs_grad(0)
    last = lax.dot_general(
        read_rows(grd[DAYS + 7 : DAYS + 8]), x[DAYS, 0:256], NT, preferred_element_type=f32
    )
    out_row = jnp.sum(last + accA[1024:1040], axis=0, keepdims=True)
    for j in range(2):
        accB[1, j, 11:12] = out_row[:, j * 128 : (j + 1) * 128]
    core_b = cp(accB.at[1 - p.r], bufB, core)

    plane_in = []
    for c in range(PARTS):
        core_in[c].wait_recv()
        for k in range(0, PROWS, 64):
            accA[rows(own + c * PROWS + k, 64)] += bufA[c * PROWS + k : c * PROWS + k + 64]
        batch = []
        for d in PLANE:
            device, q = p.plane(d)
            part = accA.at[rows(own + c * PROWS + q * OWNED, OWNED)]
            batch.append((part, rsA.at[c, d - 1], device))
        plane_in.append(cp.many(batch, rsA.at[c]))
    core_b.wait_recv()
    accB[p.r] += bufB[...]
    batch = []
    for d in LINE:
        device, z = p.line(d)
        batch.append((accB.at[p.r, z], zB.at[d - 1], device))
    line_b = cp.many(batch, zB)

    for copy in flow_in:
        copy.wait_recv()
    fS[2, 0:16] = convolve(uh, runoff + inflow(1), pad)
    flow_in = send_flow(2)

    line_in = []
    for c in range(PARTS):
        plane_in[c].wait_recv()
        total = accA[rows(own + c * PROWS + p.q * OWNED, OWNED)]
        for d in range(1, 16):
            total = total + rsA[c, d - 1]
        zA[c, p.z] = total
        mine = zA.at[c, p.z]
        line_in.append(
            cp.many([(mine, mine, p.line(d)[0]) for d in LINE], rsA.at[c, 0:7])
        )
    line_b.wait_recv()
    total = accB[p.r, p.z]
    for d in range(1, 8):
        total = total + zB[d - 1]
    xyB[p.q] = total
    mine = xyB.at[p.q]
    plane_b = cp.many([(mine, mine, p.plane(d)[0]) for d in PLANE], xyB.at[0:15])

    for copy in flow_in:
        copy.wait_recv()
    o_flow[...] = convolve(uh, runoff + inflow(2), pad)

    factor = jnp.where(p.r == 0, 0.0625, 0.125).astype(f32)
    gathered = []
    passed = []
    for c in range(PARTS):
        line_in[c].wait_recv()
        total = zA[c, 0]
        for z in range(1, 8):
            total = total + zA[c, z]
        mine = o_rec.at[rows(own + c * PROWS + p.q * OWNED, OWNED)]
        mine[...] = total * factor
        gathered.append(
            cp.many([(mine, mine, p.plane(d)[0]) for d in PLANE], rsA.at[c])
        )
    plane_b.wait_recv()
    total = xyB[0]
    for q in range(1, 16):
        total = total + xyB[q]
    outB[p.r, p.z] = total
    mine = outB.at[p.r, p.z]
    gathered_b = cp.many([(mine, mine, p.line(d)[0]) for d in LINE], zB)
    for c in range(PARTS):
        gathered[c].wait_recv()
        whole = o_rec.at[rows(own + c * PROWS, PROWS)]
        passed.append(cp(whole, whole, core))
    gathered_b.wait_recv()
    whole = outB.at[p.r]
    passed.append(cp(whole, whole, core))
    for copy in passed:
        copy.wait_recv()

    for j in range(8):
        s = slice(j * 128, (j + 1) * 128)
        back = 0.25 if j >= 4 else 0.125
        o_in[0:24, s] = outB[0, j] * back
        o_in[24:32, s] = outB[1, j, 0:8] * back
        o_bias[:, s] = outB[1, j, 8:9] * back
        if j < 2:
            o_out[:, s] = outB[1, j, 11:12] * 0.5
    cp.drain()


def write_out(*refs):
    copies = [
        pltpu.make_async_copy(refs[i], refs[5 + i], refs[10].at[i]) for i in range(5)
    ]
    for copy in copies:
        copy.start()
    for copy in copies:
        copy.wait()


def per_device(
    forcing, w_in, w_rec, bias, w_out, uh_shape, uh_scale, reach_tier, reach_dest, out_cot
):
    vmem = pl.BlockSpec(memory_space=VMEM)
    results = [
        jax.ShapeDtypeStruct((DAYS, REACH), f32),
        jax.ShapeDtypeStruct((FEAT, 1024), f32),
        jax.ShapeDtypeStruct((1024, HID), f32),
        jax.ShapeDtypeStruct((1, 1024), f32),
        jax.ShapeDtypeStruct((1, HID), f32),
    ]
    held = pl.pallas_call(
        kernel,
        out_shape=results,
        in_specs=[pl.BlockSpec(memory_space=pltpu.HBM)] * 9,
        out_specs=[vmem] * 5,
        scratch_shapes=[
            VMEM((FEAT, 1024), bf16),
            VMEM((1024, HID), bf16),
            VMEM((1, 1024), f32),
            VMEM((1, HID), f32),
            VMEM((1, REACH), f32),
            VMEM((1, REACH), f32),
            VMEM((1, REACH), jnp.int32),
            VMEM((DAYS, REACH), f32),
            pltpu.SemaphoreType.DMA((9,)),
            VMEM((GROWS, XROWS), bf16),
            VMEM((HID, 1024), bf16),
            VMEM((HID, 128), f32),
            VMEM((DAYS + 1, XROWS, REACH), bf16),
            VMEM((6, DAYS, HID, REACH), f32),
            VMEM((HID, REACH), f32),
            VMEM((GROWS, REACH), bf16),
            VMEM((HID, REACH), f32),
            VMEM((HID, REACH), f32),
            VMEM((24, REACH), f32),
            VMEM((24, REACH), f32),
            VMEM((GROWS, HID), f32),
            VMEM((2, 8, 24, 128), f32),
            VMEM((32, REACH), f32),
            VMEM((7, 24, REACH), f32),
            VMEM((3, REACH, REACH), bf16),
            VMEM((3, 24, REACH), f32),
            VMEM((3, 2, 24, REACH), f32),
            VMEM((512, HID), f32),
            VMEM((PARTS, 15, OWNED, HID), f32),
            VMEM((PARTS, 8, OWNED, HID), f32),
            VMEM((8, 24, 128), f32),
            VMEM((7, 24, 128), f32),
            VMEM((16, 24, 128), f32),
            VMEM((2, 8, 24, 128), f32),
            pltpu.SemaphoreType.DMA((SEMS,)),
            pltpu.SemaphoreType.DMA((SEMS,)),
        ],
        compiler_params=pltpu.CompilerParams(
            collective_id=0, has_side_effects=True, vmem_limit_bytes=50 * 2**20
        ),
        name="river",
    )(
        *(
            pltpu.with_memory_space_constraint(operand, pltpu.HBM)
            for operand in (
                forcing,
                w_in.T,
                w_rec,
                bias.reshape(1, 1024),
                w_out.reshape(1, HID),
                uh_shape.reshape(1, REACH),
                uh_scale.reshape(1, REACH),
                reach_dest.reshape(1, REACH),
                out_cot,
            )
        )
    )
    flow, g_in, g_rec, g_bias, g_out = pl.pallas_call(
        write_out,
        out_shape=results,
        in_specs=[pl.BlockSpec(memory_space=pl.ANY)] * 5,
        out_specs=[pl.BlockSpec(memory_space=pltpu.HBM)] * 5,
        compiler_params=pltpu.CompilerParams(vmem_limit_bytes=2 * 2**20),
        scratch_shapes=[pltpu.SemaphoreType.DMA((5,))],
        name="write_out",
    )(*held)
    return (flow, g_in.T, g_rec, g_bias.reshape(1024), g_out.reshape(HID))


def solution(mesh):
    placed = (
        P(None, None, ("basin", "rep")),
        P(),
        P(),
        P(),
        P(),
        P(("basin", "rep")),
        P(("basin", "rep")),
        P(("basin", "rep")),
        P(("basin", "rep")),
        P(None, ("basin", "rep")),
    )
    return jax.shard_map(
        per_device,
        mesh=mesh,
        in_specs=placed,
        out_specs=(P(None, ("basin", "rep")), P(), P(), P(), P()),
        check_vma=False,
    )
```

```python
import jax
import jax.numpy as jnp
from jax import lax
from jax.experimental import pallas as pl
from jax.experimental.pallas import tpu as pltpu
from jax.sharding import PartitionSpec as P

MESH = pl.DeviceIdType.MESH
VMEM = pltpu.VMEM
f32 = jnp.float32
bf16 = jnp.bfloat16
DAYS = 16
HID = 256
FEAT = 32
REACH = 256
UHLEN = 8
XROWS = 304
GROWS = 1040
CHUNK = 32
SEMS = 64
PARTS = 4
PROWS = 512 // PARTS
OWNED = PROWS // 16
NT = (((1,), (1,)), ((), ()))


class Place:
    def __init__(self):
        self.b = lax.axis_index("basin")
        self.r = lax.axis_index("rep")
        self.x = self.b // 32
        self.y = (self.b // 8) % 4
        self.z = self.b % 8
        self.q = self.x * 4 + self.y

    def core(self):
        return (self.b, 1 - self.r)

    def plane(self, d):
        px = lax.rem(self.x + d // 4, 4)
        py = lax.rem(self.y + d % 4, 4)
        return (px * 32 + py * 8 + self.z, self.r), px * 4 + py

    def plane_from(self, d):
        return lax.rem(self.x + 4 - d // 4, 4) * 4 + lax.rem(self.y + 4 - d % 4, 4)

    def line(self, d):
        pz = lax.rem(self.z + d, 8)
        return (self.x * 32 + self.y * 8 + pz, self.r), pz

    def line_from(self, d):
        return lax.rem(self.z + 8 - d, 8)

    def along(self, d):
        return (lax.rem(self.b + 128 + d, 128), self.r)


class Copies:
    def __init__(self, send, recv):
        self.send = send
        self.recv = recv
        self.all = []

    def describe(self, i, src, dst, device):
        return pltpu.make_async_remote_copy(
            src_ref=src,
            dst_ref=dst,
            send_sem=self.send.at[i],
            recv_sem=self.recv.at[i],
            device_id=device,
            device_id_type=MESH,
        )

    def __call__(self, src, dst, device):
        return self.many([(src, dst, device)], src)

    def many(self, copies, whole):
        i = len(self.all)
        for src, dst, device in copies:
            self.describe(i, src, dst, device).start()
        self.all.append(self.describe(i, whole, whole, copies[0][2]))
        return self.all[-1]

    def drain(self):
        for copy in self.all:
            copy.wait_send()


PLANE = sorted(range(1, 16), key=lambda d: (-min(d // 4, 4 - d // 4) - min(d % 4, 4 - d % 4), d))
LINE = (4, 3, 5, 2, 6, 1, 7)


def rows(start, size):
    return pl.ds(pl.multiple_of(start, 8), size)


def split3(v):
    hi = v.astype(bf16).astype(f32)
    mid = (v - hi).astype(bf16).astype(f32)
    return hi, mid, v - hi - mid


def hydro(shape_row, scale_row):
    lag = lax.broadcasted_iota(jnp.int32, (UHLEN, REACH), 0).astype(f32) + 1.0
    u = jnp.exp((shape_row - 1.0) * jnp.log(lag) - lag / scale_row)
    return u / jnp.sum(u, axis=0, keepdims=True)


def convolve(uh, series, pad):
    pad[8:24] = series
    total = uh[0:1] * series
    for m in range(1, UHLEN):
        total = total + uh[m : m + 1] * pad[8 - m : 24 - m]
    return total


def correlate(uh, series, pad):
    pad[8:24] = series
    total = uh[0:1] * series
    for m in range(1, UHLEN):
        total = total + uh[m : m + 1] * pad[8 + m : 24 + m]
    return total


def gather(blocks, index):
    halves = []
    for h in range(2):
        idx = jnp.broadcast_to(index[:, h * 128 : (h + 1) * 128], (8, 128))
        lane = jnp.bitwise_and(idx, 127)
        block = jnp.right_shift(idx, 7)
        total = jnp.zeros((8, 128), f32)
        for i in range(6):
            source = blocks[i // 2][:, (i % 2) * 128 : (i % 2 + 1) * 128]
            picked = jnp.take_along_axis(source, lane, axis=1)
            total = jnp.where(block == i, picked, total)
        halves.append(total)
    return jnp.concatenate(halves, 1)


def kernel(
    forcing_h, w_in_t_h, w_rec_h, bias_h, w_out_h, uh_shape_h, uh_scale_h, dest_h, cot_h,
    o_flow, o_in, o_rec, o_bias, o_out,
    w_in_t, w_rec, bias, w_out, uh_shape, uh_scale, dest, cot, load_sem,
    W, WT, wcol, x, fac, cells, gz, gh, gcn, rd, grd,
    accA, accB, pad, adj_late, adj_early, route, fS, fR,
    bufA, rsA, zA, bufB, zB, xyB, outB, send, recv,
):
    p = Place()
    cp = Copies(send, recv)

    barrier = pltpu.get_barrier_semaphore()
    partners = [p.along(d) for d in (6, 5, 4, 3, 2, 1, -6, -5, -4, -3, -2, -1)]
    partners += [p.plane(d)[0] for d in PLANE]
    partners += [p.line(d)[0] for d in LINE]
    partners += [p.core()]
    for device in partners:
        pl.semaphore_signal(barrier, inc=1, device_id=device, device_id_type=MESH)

    loads = [
        pltpu.make_async_copy(src, dst, load_sem.at[i])
        for i, (src, dst) in enumerate((
            (uh_shape_h, uh_shape), (uh_scale_h, uh_scale), (dest_h, dest), (cot_h, cot),
            (w_rec_h, w_rec), (w_in_t_h, w_in_t), (bias_h, bias), (w_out_h, w_out),
            (forcing_h, x.at[0:DAYS, 256:288]),
        ))
    ]
    for load in loads:
        load.start()

    pad[...] = jnp.zeros_like(pad)
    for load in loads[0:4]:
        load.wait()
    uh = hydro(uh_shape[...], uh_scale[...])
    dest_row = dest[...]
    linked = dest_row >= 0
    ahead = jnp.right_shift(dest_row, 9) - p.b
    index = jnp.where(linked, ahead * REACH + jnp.bitwise_and(dest_row, REACH - 1), -1)
    back = correlate(uh, cot[...], pad.at[0])
    adj_early[0] = back[0:8]
    adj_late[0, 0:8] = back[8:16]
    row8 = lax.broadcasted_iota(jnp.int32, (8, REACH), 0)
    adj_late[0, 8:16] = jnp.where(
        row8 == 0, uh_shape[...], jnp.where(row8 == 1, uh_scale[...], index.astype(f32))
    )
    fS[0, 16:24] = jnp.broadcast_to(index.astype(f32), (8, REACH))

    for load in loads[4:]:
        load.wait()

    for k in range(0, 1024, 128):
        half = 0.5 if k // 256 == 2 else 0.25
        back = 0.25 if k // 256 >= 2 else 0.125
        block = w_rec[k : k + 128].astype(f32)
        W[k : k + 128, 0:256] = (block * half).astype(bf16)
        WT[:, k : k + 128] = (block.T * back).astype(bf16)
        part = w_in_t[:, k : k + 128].astype(f32) * (2.0 * half)
        hi, mid, lo = split3(bias[:, k : k + 128] * (2.0 * half))
        row = lax.broadcasted_iota(jnp.int32, (96, 128), 0)
        rest = jnp.where(row == 0, hi, jnp.where(row == 1, mid, jnp.where(row == 2, lo, 0.0)))
        W[k : k + 128, 256:304] = jnp.concatenate([part, rest], 0).T[:, 0:48].astype(bf16)
    row16 = lax.broadcasted_iota(jnp.int32, (16, REACH), 0)
    hi, mid, lo = split3(w_out[...] * 0.5)
    W[1024:1040, 0:256] = jnp.where(
        row16 == 0, hi, jnp.where(row16 == 1, mid, jnp.where(row16 == 2, lo, 0.0))
    ).astype(bf16)
    W[1024:1040, 256:304] = jnp.zeros((16, 48), bf16)
    wcol[...] = jnp.broadcast_to(w_out[...], (128, HID)).T

    x[0, 0:256] = jnp.zeros((HID, REACH), bf16)
    ones = jnp.where(row16 < 3, 1.0, 0.0).astype(bf16)
    for t in range(DAYS):
        x[t, 288:304] = ones
    x[DAYS, 256:304] = jnp.zeros((48, REACH), bf16)
    cells[...] = jnp.zeros((HID, REACH), f32)

    def forward(t, _):
        pre = jnp.dot(W[...], x[t], preferred_element_type=f32)
        rd[pl.ds(t, 1)] = jnp.sum(pre[1024:1032], axis=0, keepdims=True)
        for c in range(0, HID, CHUNK):
            s = pl.ds(c, CHUNK)
            ti = jnp.tanh(pre[c : c + CHUNK])
            tf = jnp.tanh(pre[HID + c : HID + c + CHUNK])
            tg = jnp.tanh(pre[2 * HID + c : 2 * HID + c + CHUNK])
            to = jnp.tanh(pre[3 * HID + c : 3 * HID + c + CHUNK])
            i1 = 1.0 + ti
            f1 = 1.0 + tf
            o1 = 1.0 + to
            before = cells[s]
            cell = 0.5 * (f1 * before + i1 * tg)
            tc = jnp.tanh(cell)
            h2 = o1 * tc
            fac[0, t, s] = i1 * ((1.0 - ti) * tg)
            fac[1, t, s] = f1 * ((1.0 - tf) * before)
            fac[2, t, s] = i1 * (1.0 - tg * tg)
            fac[3, t, s] = h2 * (1.0 - to)
            fac[4, t, s] = o1 * (1.0 - tc * tc)
            fac[5, t, s] = 0.5 * f1
            cells[s] = cell
            x[t + 1, s] = h2.astype(bf16)
        return 0

    lax.fori_loop(0, 5, forward, 0)

    pl.semaphore_wait(barrier, len(partners))
    late_in = []
    for d in range(6, 0, -1):
        size = 16 if d < 5 else 8
        late_in.append(
            cp(adj_late.at[0, 0:size], adj_late.at[d, 0:size], p.along(-d))
        )
    early_in = [cp(adj_early.at[0], adj_early.at[d], p.along(-d)) for d in range(6, 0, -1)]

    lax.fori_loop(5, DAYS, forward, 0)
    last = jnp.dot(W[1024:1040], x[DAYS], preferred_element_type=f32)
    rd[DAYS : DAYS + 1] = jnp.sum(last, axis=0, keepdims=True)
    readout = rd[1 : DAYS + 1]

    runoff = jnp.maximum(readout, 0.0) + jnp.log1p(jnp.exp(-jnp.abs(readout)))
    fS[0, 0:16] = convolve(uh, runoff, pad.at[1])

    def send_flow(n):
        size = 24 if n == 0 else 16
        return [cp(fS.at[n, 0:size], fR.at[n, d - 1, 0:size], p.along(d)) for d in (2, 1)]

    flow_in = send_flow(0)

    kernels, indices = {0: uh}, {0: index}
    rate = 0.5 * jnp.tanh(0.5 * readout) + 0.5

    def adjoint(copies, buffer, first):
        start = {0: buffer[0, 0:8]}
        for d in range(6, 0, -1):
            copies[6 - d].wait_recv()
            start[d] = buffer[d, 0:8]
            if d < 5 and d not in kernels:
                kernels[d] = hydro(buffer[d, 8:9], buffer[d, 9:10])
                indices[d] = buffer[d, 10:11].astype(jnp.int32)
        level = start
        used = 4
        for count in (5, 3, 1):
            following = {}
            for j in range(count - 1, -1, -1):
                arrived = gather([level[j], level[j + 1], level[j + 2]], indices[j])
                pad[used, first : first + 8] = arrived
                total = start[j] + kernels[j][0:1] * arrived
                for m in range(1, UHLEN):
                    total = total + kernels[j][m : m + 1] * pad[used, first + m : first + m + 8]
                following[j] = total
                used += 1
            level = following
        return level[0]

    grd[16:24] = rate[8:16] * adjoint(late_in, adj_late, 16)
    grd[0:8] = jnp.zeros((8, REACH), f32)

    def inflow(n):
        total = jnp.zeros((DAYS, REACH), f32)
        for j in range(3):
            flow = fS[n, 0:16] if j == 0 else fR[n, j - 1, 0:16]
            parts = jnp.concatenate(split3(flow), 0).astype(bf16)
            moved = lax.dot_general(parts, route[j], NT, preferred_element_type=f32)
            total = total + moved[0:16] + moved[16:32] + moved[32:48]
        return total


    def elementwise(t):
        gr = grd[t + 8 : t + 9]
        for c in range(0, HID, CHUNK):
            s = pl.ds(c, CHUNK)
            ghc = jnp.concatenate([wcol[s], wcol[s]], 1) * gr
            if t < DAYS - 1:
                ghc = ghc + gh[s]
            gc = ghc * fac[4, t, s]
            if t < DAYS - 1:
                gc = gc + gcn[s]
            gz[t, c : c + CHUNK] = (gc * fac[0, t, s]).astype(bf16)
            gz[t, HID + c : HID + c + CHUNK] = (gc * fac[1, t, s]).astype(bf16)
            gz[t, 2 * HID + c : 2 * HID + c + CHUNK] = (gc * fac[2, t, s]).astype(bf16)
            gz[t, 3 * HID + c : 3 * HID + c + CHUNK] = (ghc * fac[3, t, s]).astype(bf16)
            gcn[s] = gc * fac[5, t, s]

    def read_rows(row):
        hi, mid, _ = split3(row)
        return jnp.where(row16 == 0, hi, jnp.where(row16 == 1, mid, 0.0)).astype(bf16)

    def inputs_grad():
        for k in range(4):
            total = jnp.zeros((48, 256), f32)
            for t in range(DAYS - 1, -1, -1):
                total = total + lax.dot_general(
                    x[t, 256:304],
                    gz[t, k * 256 : (k + 1) * 256],
                    NT,
                    preferred_element_type=f32,
                )
            for j in range(2):
                part = total[:, j * 128 : (j + 1) * 128]
                accB[0, 2 * k + j] = part[0:24]
                accB[1, 2 * k + j] = part[24:48]

    def carry(t):
        gh[...] = jnp.dot(WT[...], gz[t, 0:1024], preferred_element_type=f32)

    def rec_grad(t, s):
        term = lax.dot_general(gz[t, s], x[t, 0:256], NT, preferred_element_type=f32)
        accA[s] = term if t == DAYS - 1 else accA[s] + term

    own = p.r * 512
    other = (1 - p.r) * 512
    core = p.core()
    for t in range(DAYS - 1, 1, -1):
        elementwise(t)
        gz[t, 1024:1040] = read_rows(grd[t + 7 : t + 8])
        carry(t)
        rec_grad(t, slice(0, GROWS))
        if t == 11:
            grd[8:16] = rate[0:8] * adjoint(early_in, adj_early, 8)

    elementwise(1)
    rec_grad(1, rows(other, 512))
    core_in = [
        cp(accA.at[rows(other + c * PROWS, PROWS)], bufA.at[pl.ds(c * PROWS, PROWS)], core)
        for c in range(PARTS)
    ]
    rec_grad(1, rows(own, 512))
    plane_in = []
    for c in range(PARTS):
        core_in[c].wait_recv()
        for k in range(0, PROWS, 64):
            accA[rows(own + c * PROWS + k, 64)] += bufA[c * PROWS + k : c * PROWS + k + 64]
        batch = []
        for d in PLANE:
            device, q = p.plane(d)
            part = accA.at[rows(own + c * PROWS + q * OWNED, OWNED)]
            batch.append((part, rsA.at[c, d - 1], device))
        plane_in.append(cp.many(batch, rsA.at[c]))

    gz[1, 1024:1040] = read_rows(grd[8:9])
    rec_grad(1, slice(1024, GROWS))
    carry(1)
    elementwise(0)
    inputs_grad()
    last = lax.dot_general(
        read_rows(grd[DAYS + 7 : DAYS + 8]), x[DAYS, 0:256], NT, preferred_element_type=f32
    )
    out_row = jnp.sum(last + accA[1024:1040], axis=0, keepdims=True)
    for j in range(2):
        accB[1, j, 11:12] = out_row[:, j * 128 : (j + 1) * 128]
    core_b = cp(accB.at[1 - p.r], bufB, core)

    for copy in flow_in:
        copy.wait_recv()
    target = lax.broadcasted_iota(jnp.int32, (REACH, REACH), 0)
    for j in range(3):
        source = index if j == 0 else fR[0, j - 1, 16:17].astype(jnp.int32)
        route[j] = jnp.where(target == source - j * REACH, 1.0, 0.0).astype(bf16)
    fS[1, 0:16] = convolve(uh, runoff + inflow(0), pad.at[2])
    flow_in = send_flow(1)

    core_b.wait_recv()
    accB[p.r] += bufB[...]
    batch = []
    for d in LINE:
        device, z = p.line(d)
        batch.append((accB.at[p.r, z], zB.at[d - 1], device))
    line_b = cp.many(batch, zB)

    line_in = []
    for c in range(PARTS):
        plane_in[c].wait_recv()
        total = accA[rows(own + c * PROWS + p.q * OWNED, OWNED)]
        for d in range(1, 16):
            total = total + rsA[c, d - 1]
        zA[c, p.z] = total
        mine = zA.at[c, p.z]
        line_in.append(
            cp.many([(mine, mine, p.line(d)[0]) for d in LINE], rsA.at[c, 0:7])
        )
    line_b.wait_recv()
    total = accB[p.r, p.z]
    for d in range(1, 8):
        total = total + zB[d - 1]
    xyB[p.q] = total
    mine = xyB.at[p.q]
    plane_b = cp.many([(mine, mine, p.plane(d)[0]) for d in PLANE], xyB.at[0:15])

    for copy in flow_in:
        copy.wait_recv()
    fS[2, 0:16] = convolve(uh, runoff + inflow(1), pad.at[3])
    flow_in = send_flow(2)

    factor = jnp.where(p.r == 0, 0.0625, 0.125).astype(f32)
    gathered = []
    passed = []
    for c in range(PARTS):
        line_in[c].wait_recv()
        total = zA[c, 0]
        for z in range(1, 8):
            total = total + zA[c, z]
        mine = o_rec.at[rows(own + c * PROWS + p.q * OWNED, OWNED)]
        mine[...] = total * factor
        gathered.append(
            cp.many([(mine, mine, p.plane(d)[0]) for d in PLANE], rsA.at[c])
        )
    plane_b.wait_recv()
    total = xyB[0]
    for q in range(1, 16):
        total = total + xyB[q]
    outB[p.r, p.z] = total
    mine = outB.at[p.r, p.z]
    gathered_b = cp.many([(mine, mine, p.line(d)[0]) for d in LINE], zB)

    for copy in flow_in:
        copy.wait_recv()
    o_flow[...] = convolve(uh, runoff + inflow(2), pad.at[2])

    for c in range(PARTS - 1):
        gathered[c].wait_recv()
        whole = o_rec.at[rows(own + c * PROWS, PROWS)]
        passed.append(cp(whole, whole, core))
    gathered_b.wait_recv()
    whole = outB.at[p.r]
    passed_b = cp(whole, whole, core)
    gathered[PARTS - 1].wait_recv()
    whole = o_rec.at[rows(own + (PARTS - 1) * PROWS, PROWS)]
    passed.append(cp(whole, whole, core))
    passed_b.wait_recv()
    for j in range(8):
        s = slice(j * 128, (j + 1) * 128)
        back = 0.25 if j >= 4 else 0.125
        o_in[0:24, s] = outB[0, j] * back
        o_in[24:32, s] = outB[1, j, 0:8] * back
        o_bias[:, s] = outB[1, j, 8:9] * back
        if j < 2:
            o_out[:, s] = outB[1, j, 11:12] * 0.5
    cp.drain()
    for copy in passed:
        copy.wait_recv()


def write_out(*refs):
    copies = [
        pltpu.make_async_copy(refs[i], refs[5 + i], refs[10].at[i]) for i in range(5)
    ]
    for copy in copies:
        copy.start()
    for copy in copies:
        copy.wait()


def per_device(
    forcing, w_in, w_rec, bias, w_out, uh_shape, uh_scale, reach_tier, reach_dest, out_cot
):
    vmem = pl.BlockSpec(memory_space=VMEM)
    results = [
        jax.ShapeDtypeStruct((DAYS, REACH), f32),
        jax.ShapeDtypeStruct((FEAT, 1024), f32),
        jax.ShapeDtypeStruct((1024, HID), f32),
        jax.ShapeDtypeStruct((1, 1024), f32),
        jax.ShapeDtypeStruct((1, HID), f32),
    ]
    held = pl.pallas_call(
        kernel,
        out_shape=results,
        in_specs=[pl.BlockSpec(memory_space=pltpu.HBM)] * 9,
        out_specs=[vmem] * 5,
        scratch_shapes=[
            VMEM((FEAT, 1024), bf16),
            VMEM((1024, HID), bf16),
            VMEM((1, 1024), f32),
            VMEM((1, HID), f32),
            VMEM((1, REACH), f32),
            VMEM((1, REACH), f32),
            VMEM((1, REACH), jnp.int32),
            VMEM((DAYS, REACH), f32),
            pltpu.SemaphoreType.DMA((9,)),
            VMEM((GROWS, XROWS), bf16),
            VMEM((HID, 1024), bf16),
            VMEM((HID, 128), f32),
            VMEM((DAYS + 1, XROWS, REACH), bf16),
            VMEM((6, DAYS, HID, REACH), f32),
            VMEM((HID, REACH), f32),
            VMEM((DAYS, GROWS, REACH), bf16),
            VMEM((HID, REACH), f32),
            VMEM((HID, REACH), f32),
            VMEM((24, REACH), f32),
            VMEM((24, REACH), f32),
            VMEM((GROWS, HID), f32),
            VMEM((2, 8, 24, 128), f32),
            VMEM((13, 32, REACH), f32),
            VMEM((7, 16, REACH), f32),
            VMEM((7, 8, REACH), f32),
            VMEM((3, REACH, REACH), bf16),
            VMEM((3, 24, REACH), f32),
            VMEM((3, 2, 24, REACH), f32),
            VMEM((512, HID), f32),
            VMEM((PARTS, 15, OWNED, HID), f32),
            VMEM((PARTS, 8, OWNED, HID), f32),
            VMEM((8, 24, 128), f32),
            VMEM((7, 24, 128), f32),
            VMEM((16, 24, 128), f32),
            VMEM((2, 8, 24, 128), f32),
            pltpu.SemaphoreType.DMA((SEMS,)),
            pltpu.SemaphoreType.DMA((SEMS,)),
        ],
        compiler_params=pltpu.CompilerParams(
            collective_id=0, has_side_effects=True, vmem_limit_bytes=50 * 2**20
        ),
        name="river",
    )(
        *(
            pltpu.with_memory_space_constraint(operand, pltpu.HBM)
            for operand in (
                forcing,
                w_in.T,
                w_rec,
                bias.reshape(1, 1024),
                w_out.reshape(1, HID),
                uh_shape.reshape(1, REACH),
                uh_scale.reshape(1, REACH),
                reach_dest.reshape(1, REACH),
                out_cot,
            )
        )
    )
    flow, g_in, g_rec, g_bias, g_out = pl.pallas_call(
        write_out,
        out_shape=results,
        in_specs=[pl.BlockSpec(memory_space=pl.ANY)] * 5,
        out_specs=[pl.BlockSpec(memory_space=pltpu.HBM)] * 5,
        compiler_params=pltpu.CompilerParams(vmem_limit_bytes=2 * 2**20),
        scratch_shapes=[pltpu.SemaphoreType.DMA((5,))],
        name="write_out",
    )(*held)
    return (flow, g_in.T, g_rec, g_bias.reshape(1024), g_out.reshape(HID))


def solution(mesh):
    placed = (
        P(None, None, ("basin", "rep")),
        P(),
        P(),
        P(),
        P(),
        P(("basin", "rep")),
        P(("basin", "rep")),
        P(("basin", "rep")),
        P(("basin", "rep")),
        P(None, ("basin", "rep")),
    )
    return jax.shard_map(
        per_device,
        mesh=mesh,
        in_specs=placed,
        out_specs=(P(None, ("basin", "rep")), P(), P(), P(), P()),
        check_vma=False,
    )
```

```python
import jax
import jax.numpy as jnp
from jax import lax
from jax.experimental import pallas as pl
from jax.experimental.pallas import tpu as pltpu
from jax.sharding import PartitionSpec as P

MESH = pl.DeviceIdType.MESH
VMEM = pltpu.VMEM
f32 = jnp.float32
bf16 = jnp.bfloat16
DAYS = 16
HID = 256
FEAT = 32
REACH = 256
UHLEN = 8
XROWS = 304
GROWS = 1040
CHUNK = 32
SEMS = 64
PARTS = 4
PROWS = 512 // PARTS
OWNED = PROWS // 16
NT = (((1,), (1,)), ((), ()))


class Place:
    def __init__(self):
        self.b = lax.axis_index("basin")
        self.r = lax.axis_index("rep")
        self.x = self.b // 32
        self.y = (self.b // 8) % 4
        self.z = self.b % 8
        self.q = self.x * 4 + self.y

    def core(self):
        return (self.b, 1 - self.r)

    def plane(self, d):
        px = lax.rem(self.x + d // 4, 4)
        py = lax.rem(self.y + d % 4, 4)
        return (px * 32 + py * 8 + self.z, self.r), px * 4 + py

    def plane_from(self, d):
        return lax.rem(self.x + 4 - d // 4, 4) * 4 + lax.rem(self.y + 4 - d % 4, 4)

    def line(self, d):
        pz = lax.rem(self.z + d, 8)
        return (self.x * 32 + self.y * 8 + pz, self.r), pz

    def line_from(self, d):
        return lax.rem(self.z + 8 - d, 8)

    def along(self, d):
        return (lax.rem(self.b + 128 + d, 128), self.r)


class Copies:
    def __init__(self, send, recv):
        self.send = send
        self.recv = recv
        self.all = []

    def describe(self, i, src, dst, device):
        return pltpu.make_async_remote_copy(
            src_ref=src,
            dst_ref=dst,
            send_sem=self.send.at[i],
            recv_sem=self.recv.at[i],
            device_id=device,
            device_id_type=MESH,
        )

    def __call__(self, src, dst, device):
        return self.many([(src, dst, device)], src)

    def many(self, copies, whole):
        i = len(self.all)
        for src, dst, device in copies:
            self.describe(i, src, dst, device).start()
        self.all.append(self.describe(i, whole, whole, copies[0][2]))
        return self.all[-1]

    def drain(self):
        for copy in self.all:
            copy.wait_send()


PLANE = sorted(range(1, 16), key=lambda d: (-min(d // 4, 4 - d // 4) - min(d % 4, 4 - d % 4), d))
LINE = (4, 3, 5, 2, 6, 1, 7)


def rows(start, size):
    return pl.ds(pl.multiple_of(start, 8), size)


def split3(v):
    hi = v.astype(bf16).astype(f32)
    mid = (v - hi).astype(bf16).astype(f32)
    return hi, mid, v - hi - mid


def hydro(shape_row, scale_row):
    lag = lax.broadcasted_iota(jnp.int32, (UHLEN, REACH), 0).astype(f32) + 1.0
    u = jnp.exp((shape_row - 1.0) * jnp.log(lag) - lag / scale_row)
    return u / jnp.sum(u, axis=0, keepdims=True)


def convolve(uh, series, pad):
    pad[8:24] = series
    total = uh[0:1] * series
    for m in range(1, UHLEN):
        total = total + uh[m : m + 1] * pad[8 - m : 24 - m]
    return total


def correlate(uh, series, pad):
    pad[8:24] = series
    total = uh[0:1] * series
    for m in range(1, UHLEN):
        total = total + uh[m : m + 1] * pad[8 + m : 24 + m]
    return total


def gather(blocks, index):
    halves = []
    for h in range(2):
        idx = jnp.broadcast_to(index[:, h * 128 : (h + 1) * 128], (8, 128))
        lane = jnp.bitwise_and(idx, 127)
        block = jnp.right_shift(idx, 7)
        total = jnp.zeros((8, 128), f32)
        for i in range(6):
            source = blocks[i // 2][:, (i % 2) * 128 : (i % 2 + 1) * 128]
            picked = jnp.take_along_axis(source, lane, axis=1)
            total = jnp.where(block == i, picked, total)
        halves.append(total)
    return jnp.concatenate(halves, 1)


def kernel(
    forcing_h, w_in_t_h, w_rec_h, bias_h, w_out_h, uh_shape_h, uh_scale_h, dest_h, cot_h,
    o_flow, o_in, o_rec, o_bias, o_out,
    w_in_t, w_rec, bias, w_out, uh_shape, uh_scale, dest, cot, load_sem,
    W, WT, wcol, x, fac, cells, gz, gh, gcn, rd, grd,
    accA, accB, pad, adj_late, adj_early, turned, route, fS, fR,
    bufA, rsA, zA, bufB, zB, xyB, outB, accT, bufT, zT, xyT, outT, send, recv,
):
    p = Place()
    cp = Copies(send, recv)

    barrier = pltpu.get_barrier_semaphore()
    partners = [p.along(d) for d in (6, 5, 4, 3, 2, 1, -6, -5, -4, -3, -2, -1)]
    partners += [p.plane(d)[0] for d in PLANE]
    partners += [p.line(d)[0] for d in LINE]
    partners += [p.core()]
    for device in partners:
        pl.semaphore_signal(barrier, inc=1, device_id=device, device_id_type=MESH)

    loads = [
        pltpu.make_async_copy(src, dst, load_sem.at[i])
        for i, (src, dst) in enumerate((
            (uh_shape_h, uh_shape), (uh_scale_h, uh_scale), (dest_h, dest), (cot_h, cot),
            (w_rec_h, w_rec), (w_in_t_h, w_in_t), (bias_h, bias), (w_out_h, w_out),
            (forcing_h, x.at[0:DAYS, 256:288]),
        ))
    ]
    for load in loads:
        load.start()

    pad[...] = jnp.zeros_like(pad)
    for load in loads[0:4]:
        load.wait()
    uh = hydro(uh_shape[...], uh_scale[...])
    dest_row = dest[...]
    linked = dest_row >= 0
    ahead = jnp.right_shift(dest_row, 9) - p.b
    index = jnp.where(linked, ahead * REACH + jnp.bitwise_and(dest_row, REACH - 1), -1)
    back = correlate(uh, cot[...], pad.at[0])
    adj_early[0] = back[0:8]
    adj_late[0, 0:8] = back[8:16]
    row8 = lax.broadcasted_iota(jnp.int32, (8, REACH), 0)
    adj_late[0, 8:16] = jnp.where(
        row8 == 0, uh_shape[...], jnp.where(row8 == 1, uh_scale[...], index.astype(f32))
    )
    fS[0, 16:24] = jnp.broadcast_to(index.astype(f32), (8, REACH))

    for load in loads[4:]:
        load.wait()

    for k in range(0, 1024, 128):
        half = 0.5 if k // 256 == 2 else 0.25
        back = 0.25 if k // 256 >= 2 else 0.125
        block = w_rec[k : k + 128].astype(f32)
        W[k : k + 128, 0:256] = (block * half).astype(bf16)
        WT[:, k : k + 128] = (block.T * back).astype(bf16)
        part = w_in_t[:, k : k + 128].astype(f32) * (2.0 * half)
        hi, mid, lo = split3(bias[:, k : k + 128] * (2.0 * half))
        row = lax.broadcasted_iota(jnp.int32, (96, 128), 0)
        rest = jnp.where(row == 0, hi, jnp.where(row == 1, mid, jnp.where(row == 2, lo, 0.0)))
        W[k : k + 128, 256:304] = jnp.concatenate([part, rest], 0).T[:, 0:48].astype(bf16)
    row16 = lax.broadcasted_iota(jnp.int32, (16, REACH), 0)
    hi, mid, lo = split3(w_out[...] * 0.5)
    W[1024:1040, 0:256] = jnp.where(
        row16 == 0, hi, jnp.where(row16 == 1, mid, jnp.where(row16 == 2, lo, 0.0))
    ).astype(bf16)
    W[1024:1040, 256:304] = jnp.zeros((16, 48), bf16)
    wcol[...] = jnp.broadcast_to(w_out[...], (128, HID)).T

    x[0, 0:256] = jnp.zeros((HID, REACH), bf16)
    ones = jnp.where(row16 < 3, 1.0, 0.0).astype(bf16)
    for t in range(DAYS):
        x[t, 288:304] = ones
    x[DAYS, 256:304] = jnp.zeros((48, REACH), bf16)
    cells[...] = jnp.zeros((HID, REACH), f32)

    def forward(t, _):
        pre = jnp.dot(W[...], x[t], preferred_element_type=f32)
        rd[pl.ds(t, 1)] = jnp.sum(pre[1024:1032], axis=0, keepdims=True)
        for c in range(0, HID, CHUNK):
            s = pl.ds(c, CHUNK)
            ti = jnp.tanh(pre[c : c + CHUNK])
            tf = jnp.tanh(pre[HID + c : HID + c + CHUNK])
            tg = jnp.tanh(pre[2 * HID + c : 2 * HID + c + CHUNK])
            to = jnp.tanh(pre[3 * HID + c : 3 * HID + c + CHUNK])
            i1 = 1.0 + ti
            f1 = 1.0 + tf
            o1 = 1.0 + to
            before = cells[s]
            cell = 0.5 * (f1 * before + i1 * tg)
            tc = jnp.tanh(cell)
            h2 = o1 * tc
            fac[0, t, s] = i1 * ((1.0 - ti) * tg)
            fac[1, t, s] = f1 * ((1.0 - tf) * before)
            fac[2, t, s] = i1 * (1.0 - tg * tg)
            fac[3, t, s] = h2 * (1.0 - to)
            fac[4, t, s] = o1 * (1.0 - tc * tc)
            fac[5, t, s] = 0.5 * f1
            cells[s] = cell
            x[t + 1, s] = h2.astype(bf16)
        return 0

    lax.fori_loop(0, 5, forward, 0)

    pl.semaphore_wait(barrier, len(partners))
    late_in = []
    for d in range(6, 0, -1):
        size = 16 if d < 5 else 8
        late_in.append(
            cp(adj_late.at[0, 0:size], adj_late.at[d, 0:size], p.along(-d))
        )
    early_in = [cp(adj_early.at[0], adj_early.at[d], p.along(-d)) for d in range(6, 0, -1)]

    lax.fori_loop(5, DAYS, forward, 0)
    last = jnp.dot(W[1024:1040], x[DAYS], preferred_element_type=f32)
    rd[DAYS : DAYS + 1] = jnp.sum(last, axis=0, keepdims=True)
    readout = rd[1 : DAYS + 1]

    runoff = jnp.maximum(readout, 0.0) + jnp.log1p(jnp.exp(-jnp.abs(readout)))
    fS[0, 0:16] = convolve(uh, runoff, pad.at[1])

    def send_flow(n):
        size = 24 if n == 0 else 16
        return [cp(fS.at[n, 0:size], fR.at[n, d - 1, 0:size], p.along(d)) for d in (2, 1)]

    flow_in = send_flow(0)

    for t in range(1, DAYS):
        turned[t - 1] = x[t, 0:256].T

    kernels, indices = {0: uh}, {0: index}
    rate = 0.5 * jnp.tanh(0.5 * readout) + 0.5

    def adjoint(copies, buffer, first):
        start = {0: buffer[0, 0:8]}
        for d in range(6, 0, -1):
            copies[6 - d].wait_recv()
            start[d] = buffer[d, 0:8]
            if d < 5 and d not in kernels:
                kernels[d] = hydro(buffer[d, 8:9], buffer[d, 9:10])
                indices[d] = buffer[d, 10:11].astype(jnp.int32)
        level = start
        used = 4
        for count in (5, 3, 1):
            following = {}
            for j in range(count - 1, -1, -1):
                arrived = gather([level[j], level[j + 1], level[j + 2]], indices[j])
                pad[used, first : first + 8] = arrived
                total = start[j] + kernels[j][0:1] * arrived
                for m in range(1, UHLEN):
                    total = total + kernels[j][m : m + 1] * pad[used, first + m : first + m + 8]
                following[j] = total
                used += 1
            level = following
        return level[0]

    grd[16:24] = rate[8:16] * adjoint(late_in, adj_late, 16)
    grd[0:8] = jnp.zeros((8, REACH), f32)

    def inflow(n):
        total = jnp.zeros((DAYS, REACH), f32)
        for j in range(3):
            flow = fS[n, 0:16] if j == 0 else fR[n, j - 1, 0:16]
            parts = jnp.concatenate(split3(flow), 0).astype(bf16)
            moved = lax.dot_general(parts, route[j], NT, preferred_element_type=f32)
            total = total + moved[0:16] + moved[16:32] + moved[32:48]
        return total


    def elementwise(t):
        gr = grd[t + 8 : t + 9]
        for c in range(0, HID, CHUNK):
            s = pl.ds(c, CHUNK)
            ghc = jnp.concatenate([wcol[s], wcol[s]], 1) * gr
            if t < DAYS - 1:
                ghc = ghc + gh[s]
            gc = ghc * fac[4, t, s]
            if t < DAYS - 1:
                gc = gc + gcn[s]
            gz[t, c : c + CHUNK] = (gc * fac[0, t, s]).astype(bf16)
            gz[t, HID + c : HID + c + CHUNK] = (gc * fac[1, t, s]).astype(bf16)
            gz[t, 2 * HID + c : 2 * HID + c + CHUNK] = (gc * fac[2, t, s]).astype(bf16)
            gz[t, 3 * HID + c : 3 * HID + c + CHUNK] = (ghc * fac[3, t, s]).astype(bf16)
            gcn[s] = gc * fac[5, t, s]

    def read_rows(row):
        hi, mid, _ = split3(row)
        return jnp.where(row16 == 0, hi, jnp.where(row16 == 1, mid, 0.0)).astype(bf16)

    def inputs_grad(days, first):
        for k in range(4):
            total = jnp.zeros((48, 256), f32)
            for t in days:
                total = total + lax.dot_general(
                    x[t, 256:304],
                    gz[t, k * 256 : (k + 1) * 256],
                    NT,
                    preferred_element_type=f32,
                )
            for j in range(2):
                part = total[:, j * 128 : (j + 1) * 128]
                for i in range(2):
                    term = part[16 * i : 16 * i + 16]
                    accB[i, 2 * k + j] = term if first else accB[i, 2 * k + j] + term
                row = slice(2 * k + j, 2 * k + j + 1)
                accT[0, row] = part[32:33] if first else accT[0, row] + part[32:33]

    def carry(t):
        gh[...] = jnp.dot(WT[...], gz[t, 0:1024], preferred_element_type=f32)

    def rec_grad(t, s):
        term = jnp.dot(gz[t, s], turned[t - 1], preferred_element_type=f32)
        accA[s] = term if t == DAYS - 1 else accA[s] + term

    own = p.r * 512
    other = (1 - p.r) * 512
    core = p.core()
    for t in range(DAYS - 1, 1, -1):
        elementwise(t)
        gz[t, 1024:1040] = read_rows(grd[t + 7 : t + 8])
        carry(t)
        rec_grad(t, slice(0, GROWS))
        if t == 11:
            grd[8:16] = rate[0:8] * adjoint(early_in, adj_early, 8)

    elementwise(1)
    rec_grad(1, rows(other, 512))
    core_in = [
        cp(accA.at[rows(other + c * PROWS, PROWS)], bufA.at[pl.ds(c * PROWS, PROWS)], core)
        for c in range(PARTS)
    ]
    rec_grad(1, rows(own, 512))
    inputs_grad(range(15, 9, -1), True)
    plane_in = []
    for c in range(PARTS):
        core_in[c].wait_recv()
        for k in range(0, PROWS, 64):
            accA[rows(own + c * PROWS + k, 64)] += bufA[c * PROWS + k : c * PROWS + k + 64]
        batch = []
        for d in PLANE:
            device, q = p.plane(d)
            part = accA.at[rows(own + c * PROWS + q * OWNED, OWNED)]
            batch.append((part, rsA.at[c, d - 1], device))
        plane_in.append(cp.many(batch, rsA.at[c]))

    gz[1, 1024:1040] = read_rows(grd[8:9])
    rec_grad(1, slice(1024, GROWS))
    carry(1)
    elementwise(0)
    inputs_grad(range(9, -1, -1), False)
    last = lax.dot_general(
        read_rows(grd[DAYS + 7 : DAYS + 8]), x[DAYS, 0:256], NT, preferred_element_type=f32
    )
    out_row = jnp.sum(last + accA[1024:1040], axis=0, keepdims=True)
    accT[1] = jnp.zeros((8, 128), f32)
    for j in range(2):
        accT[1, j : j + 1] = out_row[:, j * 128 : (j + 1) * 128]
    core_b = cp(accB.at[1 - p.r], bufB, core)
    core_t = cp(accT.at[1 - p.r], bufT, core)

    for copy in flow_in:
        copy.wait_recv()
    target = lax.broadcasted_iota(jnp.int32, (REACH, REACH), 0)
    for j in range(3):
        source = index if j == 0 else fR[0, j - 1, 16:17].astype(jnp.int32)
        route[j] = jnp.where(target == source - j * REACH, 1.0, 0.0).astype(bf16)
    fS[1, 0:16] = convolve(uh, runoff + inflow(0), pad.at[2])
    flow_in = send_flow(1)

    core_b.wait_recv()
    accB[p.r] += bufB[...]
    batch = []
    for d in LINE:
        device, z = p.line(d)
        batch.append((accB.at[p.r, z], zB.at[d - 1], device))
    line_b = cp.many(batch, zB)
    core_t.wait_recv()
    zT[p.z] = accT[p.r] + bufT[...]
    mine = zT.at[p.z]
    line_t = cp.many([(mine, mine, p.line(d)[0]) for d in LINE], zT.at[0:7])

    line_in = []
    for c in range(PARTS):
        plane_in[c].wait_recv()
        total = accA[rows(own + c * PROWS + p.q * OWNED, OWNED)]
        for d in range(1, 16):
            total = total + rsA[c, d - 1]
        zA[c, p.z] = total
        mine = zA.at[c, p.z]
        line_in.append(
            cp.many([(mine, mine, p.line(d)[0]) for d in LINE], rsA.at[c, 0:7])
        )
    line_b.wait_recv()
    total = accB[p.r, p.z]
    for d in range(1, 8):
        total = total + zB[d - 1]
    xyB[p.q] = total
    mine = xyB.at[p.q]
    plane_b = cp.many([(mine, mine, p.plane(d)[0]) for d in PLANE], xyB.at[0:15])
    line_t.wait_recv()
    total = zT[0]
    for z in range(1, 8):
        total = total + zT[z]
    xyT[p.q] = total
    mine = xyT.at[p.q]
    plane_t = cp.many([(mine, mine, p.plane(d)[0]) for d in PLANE], xyT.at[0:15])

    for copy in flow_in:
        copy.wait_recv()
    fS[2, 0:16] = convolve(uh, runoff + inflow(1), pad.at[3])
    flow_in = send_flow(2)

    factor = jnp.where(p.r == 0, 0.0625, 0.125).astype(f32)
    gathered = []
    passed = []
    for c in range(PARTS):
        line_in[c].wait_recv()
        total = zA[c, 0]
        for z in range(1, 8):
            total = total + zA[c, z]
        mine = o_rec.at[rows(own + c * PROWS + p.q * OWNED, OWNED)]
        mine[...] = total * factor
        gathered.append(
            cp.many([(mine, mine, p.plane(d)[0]) for d in PLANE], rsA.at[c])
        )
    plane_b.wait_recv()
    total = xyB[0]
    for q in range(1, 16):
        total = total + xyB[q]
    outB[p.r, p.z] = total
    mine = outB.at[p.r, p.z]
    gathered_b = cp.many([(mine, mine, p.line(d)[0]) for d in LINE], zB)
    plane_t.wait_recv()
    total = xyT[0]
    for q in range(1, 16):
        total = total + xyT[q]
    outT[p.r] = total
    mine = outT.at[p.r]
    passed_t = cp(mine, mine, core)

    for copy in flow_in:
        copy.wait_recv()
    o_flow[...] = convolve(uh, runoff + inflow(2), pad.at[2])

    for c in range(PARTS - 1):
        gathered[c].wait_recv()
        whole = o_rec.at[rows(own + c * PROWS, PROWS)]
        passed.append(cp(whole, whole, core))
    gathered_b.wait_recv()
    whole = outB.at[p.r]
    passed_b = cp(whole, whole, core)
    gathered[PARTS - 1].wait_recv()
    whole = o_rec.at[rows(own + (PARTS - 1) * PROWS, PROWS)]
    passed.append(cp(whole, whole, core))
    passed_t.wait_recv()
    passed_b.wait_recv()
    for j in range(8):
        s = slice(j * 128, (j + 1) * 128)
        back = 0.25 if j >= 4 else 0.125
        o_in[0:16, s] = outB[0, j] * back
        o_in[16:32, s] = outB[1, j] * back
        o_bias[:, s] = outT[0, j : j + 1] * back
        if j < 2:
            o_out[:, s] = outT[1, j : j + 1] * 0.5
    cp.drain()
    for copy in passed:
        copy.wait_recv()


def write_out(*refs):
    copies = [
        pltpu.make_async_copy(refs[i], refs[5 + i], refs[10].at[i]) for i in range(5)
    ]
    for copy in copies:
        copy.start()
    for copy in copies:
        copy.wait()


def per_device(
    forcing, w_in, w_rec, bias, w_out, uh_shape, uh_scale, reach_tier, reach_dest, out_cot
):
    vmem = pl.BlockSpec(memory_space=VMEM)
    results = [
        jax.ShapeDtypeStruct((DAYS, REACH), f32),
        jax.ShapeDtypeStruct((FEAT, 1024), f32),
        jax.ShapeDtypeStruct((1024, HID), f32),
        jax.ShapeDtypeStruct((1, 1024), f32),
        jax.ShapeDtypeStruct((1, HID), f32),
    ]
    held = pl.pallas_call(
        kernel,
        out_shape=results,
        in_specs=[pl.BlockSpec(memory_space=pltpu.HBM)] * 9,
        out_specs=[vmem] * 5,
        scratch_shapes=[
            VMEM((FEAT, 1024), bf16),
            VMEM((1024, HID), bf16),
            VMEM((1, 1024), f32),
            VMEM((1, HID), f32),
            VMEM((1, REACH), f32),
            VMEM((1, REACH), f32),
            VMEM((1, REACH), jnp.int32),
            VMEM((DAYS, REACH), f32),
            pltpu.SemaphoreType.DMA((9,)),
            VMEM((GROWS, XROWS), bf16),
            VMEM((HID, 1024), bf16),
            VMEM((HID, 128), f32),
            VMEM((DAYS + 1, XROWS, REACH), bf16),
            VMEM((6, DAYS, HID, REACH), f32),
            VMEM((HID, REACH), f32),
            VMEM((DAYS, GROWS, REACH), bf16),
            VMEM((HID, REACH), f32),
            VMEM((HID, REACH), f32),
            VMEM((24, REACH), f32),
            VMEM((24, REACH), f32),
            VMEM((GROWS, HID), f32),
            VMEM((2, 8, 16, 128), f32),
            VMEM((13, 32, REACH), f32),
            VMEM((7, 16, REACH), f32),
            VMEM((7, 8, REACH), f32),
            VMEM((DAYS - 1, REACH, HID), bf16),
            VMEM((3, REACH, REACH), bf16),
            VMEM((3, 24, REACH), f32),
            VMEM((3, 2, 24, REACH), f32),
            VMEM((512, HID), f32),
            VMEM((PARTS, 15, OWNED, HID), f32),
            VMEM((PARTS, 8, OWNED, HID), f32),
            VMEM((8, 16, 128), f32),
            VMEM((7, 16, 128), f32),
            VMEM((16, 16, 128), f32),
            VMEM((2, 8, 16, 128), f32),
            VMEM((2, 8, 128), f32),
            VMEM((8, 128), f32),
            VMEM((8, 8, 128), f32),
            VMEM((16, 8, 128), f32),
            VMEM((2, 8, 128), f32),
            pltpu.SemaphoreType.DMA((SEMS,)),
            pltpu.SemaphoreType.DMA((SEMS,)),
        ],
        compiler_params=pltpu.CompilerParams(
            collective_id=0, has_side_effects=True, vmem_limit_bytes=50 * 2**20
        ),
        name="river",
    )(
        *(
            pltpu.with_memory_space_constraint(operand, pltpu.HBM)
            for operand in (
                forcing,
                w_in.T,
                w_rec,
                bias.reshape(1, 1024),
                w_out.reshape(1, HID),
                uh_shape.reshape(1, REACH),
                uh_scale.reshape(1, REACH),
                reach_dest.reshape(1, REACH),
                out_cot,
            )
        )
    )
    flow, g_in, g_rec, g_bias, g_out = pl.pallas_call(
        write_out,
        out_shape=results,
        in_specs=[pl.BlockSpec(memory_space=pl.ANY)] * 5,
        out_specs=[pl.BlockSpec(memory_space=pltpu.HBM)] * 5,
        compiler_params=pltpu.CompilerParams(vmem_limit_bytes=2 * 2**20),
        scratch_shapes=[pltpu.SemaphoreType.DMA((5,))],
        name="write_out",
    )(*held)
    return (flow, g_in.T, g_rec, g_bias.reshape(1024), g_out.reshape(HID))


def solution(mesh):
    placed = (
        P(None, None, ("basin", "rep")),
        P(),
        P(),
        P(),
        P(),
        P(("basin", "rep")),
        P(("basin", "rep")),
        P(("basin", "rep")),
        P(("basin", "rep")),
        P(None, ("basin", "rep")),
    )
    return jax.shard_map(
        per_device,
        mesh=mesh,
        in_specs=placed,
        out_specs=(P(None, ("basin", "rep")), P(), P(), P(), P()),
        check_vma=False,
    )
```
